256 devices in a mesh: seq: 32 (over y_lo, z, core), head: 8 (over x, y_hi).
Axes of the slice: x: 4, y: 4 (y_hi: 2, y_lo: 2; y = y_hi * 2 + y_lo), z: 8, core: 2. Of those that a mesh axis runs over, the one named last changes fastest.
Arguments:
- span_qkv: bfloat16 [3, 8192, 4096], P(None, ('seq', 'head')), may hold values from -35 to 35
- cache_kv: bfloat16 [2, 4096, 4096], P(None, 'seq', 'head'), may hold values from -6 to 6
- audio_kv: bfloat16 [2, 512, 4096], P(None, None, 'head'), may hold values from -35 to 35
- video_kv: bfloat16 [2, 512, 4096], P(None, None, 'head'), may hold values from -35 to 35
- block_mask: int32 [8, 128, 192], P('head'), may hold values 0 or 1
- mem_lengths: int32 [2], replicated, may hold values from 128 to 512, as said below
- cross_gates: float32 [2, 32], P(None, 'head'), may hold values from -2 to 2
- out_weight: bfloat16 [4096, 4096], P('head'), may hold values from -1 to 1
Outputs:
- attn_out: bfloat16 [8192, 4096], P(('seq', 'head'))
The draws below stay inside these ranges and needn't reach their ends.
Inputs may be any that keep to these rules, and one draw needn't show every extreme that they name: `mem_lengths`: one of the two lengths is 512.
All inputs are finite; a program needn't handle non-finite values. No bound on the sum of `block_mask` on one device may be relied on, other than what follows from the above.
Results may differ from the reference program's by a relative error of at most 0.019.
Values may be sent and summed in bfloat16 or wider, within the bound.
No kernel may reach another device: no remote copies, remote signals or barrier semaphores. Data moves between devices by JAX's collectives and lax.ppermute only.
A program may use at most 128 MiB of HBM per device.

```python
import math
import jax
import jax.numpy as jnp
from jax import lax

D = 4096
H = 32
HD = 128
G = 8
BLK = 64
CH_DEV = 256
MEM = 512
SPAN = 8192
CTX = 4096
NQB = 128
NKB = 192
N_SEQ = 32
N_HEAD = 8


def memory_draw(key):
    values = jnp.clip(jax.random.normal(key, (2, MEM, H * HD), jnp.float32), -6.0, 6.0)
    return values.astype(jnp.bfloat16)


def draw_span_qkv(key, part):
    key = jax.random.fold_in(key, 1)
    values = jnp.clip(jax.random.normal(key, (3, SPAN, H * HD), jnp.float32), -6.0, 6.0)
    return values.astype(jnp.bfloat16)


def draw_audio_kv(key, part):
    key = jax.random.fold_in(key, 2)
    return memory_draw(key)


def draw_video_kv(key, part):
    key = jax.random.fold_in(key, 3)
    return memory_draw(key)


def draw_mem_lengths(key, part):
    key = jax.random.fold_in(key, 4)
    first_key, second_key = jax.random.split(key)
    length = jax.random.randint(first_key, (), MEM // 4, MEM + 1)
    chosen = jax.random.randint(second_key, (), 0, 2)
    return jnp.where(jnp.arange(2) == chosen, MEM, length).astype(jnp.int32)


def plant(result, stream_key, low, high):
    spot = [jax.random.randint(jax.random.fold_in(stream_key, axis), (), 0, length) for axis, length in enumerate(result.shape)]
    longest = result.shape.index(max(result.shape))
    next_to = spot[:longest] + [(spot[longest] + 1) % result.shape[longest]] + spot[longest + 1:]
    return result.at[tuple(spot)].set(low).at[tuple(next_to)].set(high)


def block_scale(own_key, shape, cuts, least, high):
    factor_of, own = 1.0, jax.random.fold_in(own_key, 6)
    for position, blocks in cuts:
        heights = jnp.exp(jax.random.uniform(jax.random.fold_in(own, position), (blocks,), jnp.float32, least / len(cuts), high / len(cuts)))
        factor_of = factor_of * jnp.repeat(heights, shape[position] // blocks).reshape([-1 if axis == position else 1 for axis in range(len(shape))])
    return factor_of


def noise(stream_key, extent, deviation, reach, cuts=(), kind=jnp.bfloat16):
    factor_of = block_scale(stream_key, extent, cuts, -0.22, 0.18) if cuts else 1.0
    drawn = jax.random.normal(stream_key, extent, jnp.float32) * deviation * factor_of
    return jnp.minimum(jnp.maximum(drawn, -reach), reach).astype(kind)


def setup_inputs(seed: int = 0) -> dict:
    key_of = jax.random.split(jax.random.key(seed), 9)
    span_qkv = draw_span_qkv(jax.random.fold_in(key_of[8], 71), 0)
    cache_kv = noise(key_of[1], (2, CTX, H * HD), 1.0, 6.0, ((1, 32), (2, 8)))
    audio_kv = draw_audio_kv(jax.random.fold_in(key_of[8], 71), 0)
    video_kv = draw_video_kv(jax.random.fold_in(key_of[8], 71), 0)
    block_mask = plant((jax.random.randint(key_of[4], (G, NQB, NKB), 0, 4) < 1).astype(jnp.int32), jax.random.fold_in(key_of[4], 1), 0, 1)
    mem_lengths = draw_mem_lengths(jax.random.fold_in(key_of[8], 71), 0)
    cross_gates = jnp.clip(jax.random.uniform(key_of[6], (2, H), jnp.float32, -2.0, 2.0) * block_scale(key_of[6], (2, H), ((1, 8),), -0.4, 0.0), -2.0, 2.0)
    out_weight = noise(key_of[7], (H * HD, D), H ** -0.5, 1.0, ((0, 8),))
    return dict(span_qkv=span_qkv, cache_kv=cache_kv, audio_kv=audio_kv, video_kv=video_kv, block_mask=block_mask, mem_lengths=mem_lengths, cross_gates=cross_gates, out_weight=out_weight)


neg_large = -1e+30

def seq_positions(storage, dev_count, per_dev):
    half_len = per_dev // 2
    device = storage // per_dev
    within = storage % per_dev
    segment = jnp.where(within < half_len, device, 2 * dev_count - 1 - device)
    return (segment * half_len + within % half_len).astype(jnp.int32)

def masked_softmax_rows(scores, allowed, values):
    row_top = lax.optimization_barrier(jnp.max(jnp.where(allowed, scores, neg_large), axis=1, keepdims=True))
    weights = jnp.where(allowed, jnp.exp(scores - row_top), 0.0)
    row_total = lax.optimization_barrier(jnp.sum(weights, axis=1, keepdims=True))
    product = jnp.dot(weights.astype(jnp.bfloat16), values, preferred_element_type=jnp.float32)
    return product / row_total

def reference(span_qkv, cache_kv, audio_kv, video_kv, block_mask, mem_lengths, cross_gates, out_weight):
    score_scale = 1.0 / math.sqrt(HD)
    per_group = H // G
    cache_count = CTX // BLK
    positions = seq_positions(jnp.arange(SPAN, dtype=jnp.int32), N_SEQ, CH_DEV)
    span_blocks = positions // BLK
    cache_blocks = jnp.arange(CTX, dtype=jnp.int32) // BLK
    key_all = jnp.concatenate([cache_kv[0], span_qkv[1]], axis=0)
    value_all = jnp.concatenate([cache_kv[1], span_qkv[2]], axis=0)
    slot_ids = jnp.arange(MEM, dtype=jnp.int32)
    row_step = 512

    def one_head(head_index):
        group_index = head_index // per_group
        mask_group = block_mask[group_index]
        first_col = head_index * HD
        head_queries = lax.dynamic_slice_in_dim(span_qkv[0], first_col, HD, 1)
        head_keys = lax.dynamic_slice_in_dim(key_all, first_col, HD, 1)
        head_values = lax.dynamic_slice_in_dim(value_all, first_col, HD, 1)
        audio_keys = lax.dynamic_slice_in_dim(audio_kv[0], first_col, HD, 1)
        audio_values = lax.dynamic_slice_in_dim(audio_kv[1], first_col, HD, 1)
        video_keys = lax.dynamic_slice_in_dim(video_kv[0], first_col, HD, 1)
        video_values = lax.dynamic_slice_in_dim(video_kv[1], first_col, HD, 1)
        gate_audio = jnp.tanh(cross_gates[0, head_index])
        gate_video = jnp.tanh(cross_gates[1, head_index])

        def one_block(first_row):
            query_rows = lax.dynamic_slice_in_dim(head_queries, first_row, row_step, 0)
            query_pos = lax.dynamic_slice_in_dim(positions, first_row, row_step, 0)
            query_blocks = query_pos // BLK
            mask_rows = jnp.take(mask_group, query_blocks, axis=0)
            cache_ok = jnp.take(mask_rows, cache_blocks, axis=1) != 0
            span_ok = jnp.take(mask_rows, cache_count + span_blocks, axis=1) != 0
            same_block = span_blocks[None, :] == query_blocks[:, None]
            causal = positions[None, :] <= query_pos[:, None]
            allowed = jnp.concatenate([cache_ok, causal & (same_block | span_ok)], axis=1)
            scores = jnp.dot(query_rows, head_keys.T, preferred_element_type=jnp.float32) * score_scale
            own_attn = masked_softmax_rows(scores, allowed, head_values)
            audio_scores = jnp.dot(query_rows, audio_keys.T, preferred_element_type=jnp.float32) * score_scale
            audio_live = jnp.broadcast_to(slot_ids[None, :] < mem_lengths[0], audio_scores.shape)
            audio_part = masked_softmax_rows(audio_scores, audio_live, audio_values)
            video_scores = jnp.dot(query_rows, video_keys.T, preferred_element_type=jnp.float32) * score_scale
            video_live = jnp.broadcast_to(slot_ids[None, :] < mem_lengths[1], video_scores.shape)
            video_part = masked_softmax_rows(video_scores, video_live, video_values)
            return own_attn + gate_audio * audio_part + gate_video * video_part
        blocks_out = lax.map(one_block, jnp.arange(0, SPAN, row_step, dtype=jnp.int32))
        return blocks_out.reshape(SPAN, HD)
    heads_out = lax.map(one_head, jnp.arange(H, dtype=jnp.int32))
    mixed = jnp.transpose(heads_out, (1, 0, 2)).reshape(SPAN, H * HD).astype(jnp.bfloat16)
    group_cols = H * HD // N_HEAD

    def add_partial(group_index, total):
        first_col = (group_index * group_cols).astype(jnp.int32)
        piece = lax.dynamic_slice_in_dim(mixed, first_col, group_cols, 1)
        rows = lax.dynamic_slice_in_dim(out_weight, first_col, group_cols, 0)
        partial_sum = jnp.dot(piece, rows, preferred_element_type=jnp.float32).astype(jnp.bfloat16)
        partial_sum = lax.optimization_barrier(partial_sum)
        return total + partial_sum.astype(jnp.float32)
    total = lax.fori_loop(0, N_HEAD, add_partial, jnp.zeros((SPAN, D), jnp.float32))
    return total.astype(jnp.bfloat16)
```

```python
import functools
import math

import jax
import jax.numpy as jnp
from jax import lax
from jax.experimental import pallas as pl
from jax.experimental.pallas import tpu as pltpu
from jax.sharding import Mesh
from jax.sharding import PartitionSpec as P

HD = 128
neg_large = -1e30
score_scale = math.log2(math.e) / math.sqrt(HD)

AXES = ("yl", "z2", "z1", "z0", "c", "x", "yh")
SIZES = (2, 2, 2, 2, 2, 4, 2)
ZZ = ("z2", "z1")
HEADS = ("x", "yh")

VM = pltpu.VMEM
SM = pltpu.SMEM
whole = functools.partial(pl.BlockSpec, memory_space=VM)
scalars = functools.partial(pl.BlockSpec, memory_space=SM)
params = functools.partial(pltpu.CompilerParams, vmem_limit_bytes=40 * 2**20)


def xor_perm(count, k):
    return [(i, i ^ k) for i in range(count)]


def pack_kernel(where_ref, span_ref, cache_ref, span_out, cache_out):
    j = where_ref[1]
    for d in range(32):
        col = ((d % 8) * 4 + d // 8) * HD
        span_out[d] = span_ref[:, :, col:col + HD]
    for k in range(4):
        col = pl.multiple_of((j ^ k) * HD, HD)
        cache_out[k] = cache_ref[:, :, pl.ds(col, HD)]


def unpack_kernel(got_ref, q_out, kv_out):
    for t in range(8):
        first = (t if t < 4 else 7 - t) * 8 + (t // 4) * 4
        rows = slice(t * 128, (t + 1) * 128)
        q_out[rows, :] = got_ref[first:first + 4, 0].reshape(128, HD)
        kv_out[0, rows, :] = got_ref[first:first + 4, 1].reshape(128, HD)
        kv_out[1, rows, :] = got_ref[first:first + 4, 2].reshape(128, HD)


def segment_of(t, yl, z0, c):
    low = t < 4
    s = yl * 16 + jnp.where(low, t, 7 - t) * 4 + z0 * 2 + c
    return jnp.where(low, s, 63 - s)


def bias_kernel(where_ref, mask_ref, cache_out, *span_outs):
    yl, j, z0, c = where_ref[0], where_ref[1], where_ref[2], where_ref[3]
    mask = mask_ref[0].astype(jnp.float32).astype(jnp.bfloat16)
    r = lax.broadcasted_iota(jnp.int32, (16, 128), 0)
    qb = 2 * segment_of(r >> 1, yl, z0, c) + (r & 1)
    pick = (lax.broadcasted_iota(jnp.int32, (16, 128), 1) == qb).astype(jnp.float32)
    rows = jnp.dot(pick.astype(jnp.bfloat16), mask, preferred_element_type=jnp.float32)
    rows = rows.astype(jnp.bfloat16)

    def spread(block):
        n = block.shape[1]
        one = lax.broadcasted_iota(jnp.int32, (192, n), 0) == jnp.broadcast_to(block, (192, n))
        one = jnp.where(one, 1.0, 0.0).astype(jnp.bfloat16)
        return jnp.dot(rows, one, preferred_element_type=jnp.float32) > 0.5

    for g in range(4):
        dy, dz = g >> 1, g & 1
        lane = lax.broadcasted_iota(jnp.int32, (1, 1024), 1)
        dc, k, b = lane >> 9, (lane >> 7) & 3, (lane >> 6) & 1
        s = (yl ^ dy) * 16 + (j ^ k) * 4 + (z0 ^ dz) * 2 + (c ^ dc)
        ok = spread(2 * s + b)
        cache_out[:, g * 1024:(g + 1) * 1024] = jnp.where(ok, 0.0, neg_large)
        for half in range(2):
            t, b = lane >> 7, (lane >> 6) & 1
            kb = 2 * segment_of(t, yl ^ dy, z0 ^ dz, c ^ half) + b
            ok = spread(kb + 64).astype(jnp.int32)
            q_full = jnp.broadcast_to(qb[:, :1], (16, 1024))
            k_full = jnp.broadcast_to(kb, (16, 1024))
            ok = ((k_full < q_full) & (ok != 0)) | (k_full == q_full)
            span_outs[g][:, half * 1024:(half + 1) * 1024] = jnp.where(ok, 0.0, neg_large)


def score_tile(q, keys):
    return lax.dot_general(
        q, keys, (((1,), (1,)), ((), ())), preferred_element_type=jnp.float32
    )


def lane_sums(p):
    total = p[:, :HD]
    for i in range(1, p.shape[1] // HD):
        total = total + p[:, i * HD:(i + 1) * HD]
    return total


def fold(state, q, keys, values, bias_ref, block, lanes, causal=None):
    top, total, acc = state
    raw = score_tile(q, keys) * score_scale
    parts = []
    for i in range(q.shape[0] // 64):
        parts.append(raw[i * 64:(i + 1) * 64] + bias_ref[pl.ds(block + i, 1), lanes])
    s = jnp.concatenate(parts, axis=0)
    if causal is not None:
        s = s + causal
    new_top = jnp.maximum(top, jnp.max(s, axis=1, keepdims=True))
    factor = jnp.exp2(top - new_top)
    p = jnp.exp2(s - new_top[:, :1])
    total = total * factor + lane_sums(p)
    acc = acc * factor + jnp.dot(
        p.astype(jnp.bfloat16), values, preferred_element_type=jnp.float32
    )
    return new_top, total, acc


def cache_kernel(q_ref, *refs):
    kv, bias_ref, top_out, total_out, acc_out = refs[:8], refs[8], refs[9], refs[10], refs[11]

    def step(w, _):
        rows = pl.ds(pl.multiple_of(w * 256, 256), 256)
        q = q_ref[rows, :]
        state = (
            jnp.full((256, HD), neg_large, jnp.float32),
            jnp.zeros((256, HD), jnp.float32),
            jnp.zeros((256, HD), jnp.float32),
        )
        for n in range(8):
            state = fold(
                state, q, kv[n][:, 0].reshape(512, HD), kv[n][:, 1].reshape(512, HD),
                bias_ref, w * 4, slice(n * 512, (n + 1) * 512),
            )
        top_out[rows, :], total_out[rows, :], acc_out[rows, :] = state
        return 0

    lax.fori_loop(0, 4, step, 0)


def memory_kernel(where_ref, len_ref, gate_ref, q_ref, audio_ref, video_ref, out_ref):
    j = where_ref[1]
    slot = lax.broadcasted_iota(jnp.int32, (1, 512), 1)

    def step(w, _):
        rows = pl.ds(pl.multiple_of(w * 256, 256), 256)
        q = q_ref[rows, :]
        mixed = jnp.zeros((256, HD), jnp.float32)
        for n, mem_ref in enumerate((audio_ref, video_ref)):
            bias = jnp.where(slot < len_ref[n], 0.0, neg_large)
            s = score_tile(q, mem_ref[0]) * score_scale + bias
            p = jnp.exp2(s - jnp.max(s, axis=1, keepdims=True))
            total = jnp.sum(p, axis=1, keepdims=True)
            part = jnp.dot(
                p.astype(jnp.bfloat16), mem_ref[1], preferred_element_type=jnp.float32
            )
            gate = jnp.tanh(jnp.full((1, HD), gate_ref[n, j], jnp.float32))
            mixed = mixed + gate * (part / total)
        out_ref[rows, :] = mixed
        return 0

    lax.fori_loop(0, 4, step, 0)


def span_kernel(own, last, where_ref, q_ref, kv0_ref, kv1_ref, bias_ref, *refs):
    top_ref, total_ref, acc_ref = refs[:3]
    if last:
        extra_ref, out_ref = refs[3:]
    else:
        outs = refs[3:]
    j = where_ref[1]
    for w in range(4):
        rows = slice(w * 256, (w + 1) * 256)
        q = q_ref[rows, :]
        state = (top_ref[rows, :], total_ref[rows, :], acc_ref[rows, :])
        for dc, kv_ref in enumerate((kv0_ref, kv1_ref)):
            for half in range(1 if w < 2 else 2):
                keys = slice(half * 512, (half + 1) * 512)
                causal = None
                if own and dc == 0:
                    row = lax.broadcasted_iota(jnp.int32, (256, 512), 0) + w * 256
                    col = lax.broadcasted_iota(jnp.int32, (256, 512), 1) + half * 512
                    causal = jnp.where(col <= row, 0.0, neg_large)
                state = fold(
                    state, q, kv_ref[0, keys, :], kv_ref[1, keys, :], bias_ref, w * 4,
                    slice(dc * 1024 + half * 512, dc * 1024 + (half + 1) * 512), causal,
                )
        if last:
            top, total, acc = state
            mixed = acc / jnp.sum(total, axis=1, keepdims=True) + extra_ref[rows, :]
            mixed = mixed.astype(jnp.bfloat16)
            for i in range(2):
                t = w * 2 + i
                to = t if t < 4 else 7 - t
                half = t // 4
                out_ref[j ^ to, half * 128:(half + 1) * 128, :] = mixed[i * 128:(i + 1) * 128]
        else:
            outs[0][rows, :], outs[1][rows, :], outs[2][rows, :] = state


def project_kernel(where_ref, m0, m1, m2, m3, w_ref, out_ref, mixed):
    j = where_ref[1]

    @pl.when(pl.program_id(0) == 0)
    def _():
        for k, m in enumerate((m0, m1, m2, m3)):
            mixed[:, pl.ds(pl.multiple_of((j ^ k) * HD, HD), HD)] = m[...]

    part = jnp.dot(mixed[...], w_ref[...], preferred_element_type=jnp.float32)
    part = part.astype(jnp.bfloat16)
    for h in range(8):
        out_ref[h] = part[h * 32:(h + 1) * 32]


def cost(flops, size, exps=0):
    return pl.CostEstimate(flops=flops, bytes_accessed=size, transcendentals=exps)


def f32(*shape):
    return jax.ShapeDtypeStruct(shape, jnp.float32)


def b16(*shape):
    return jax.ShapeDtypeStruct(shape, jnp.bfloat16)


def shards(
    span_qkv, cache_kv, audio_kv, video_kv, block_mask, mem_lengths, cross_gates, out_weight
):
    j = lax.axis_index("z2") * 2 + lax.axis_index("z1")
    where = jnp.stack(
        [lax.axis_index("yl"), j, lax.axis_index("z0"), lax.axis_index("c")]
    ).astype(jnp.int32)

    span_packed, cache_packed = pl.pallas_call(
        pack_kernel,
        out_shape=(b16(32, 3, 32, HD), b16(4, 2, 128, HD)),
        in_specs=[scalars(), whole(), whole()],
        out_specs=(whole(), whole()),
        compiler_params=params(),
        cost_estimate=cost(0, 4 * 2**20),
        name="pack",
    )(where, span_qkv, cache_kv)

    cache_own = [cache_packed[0]] + [
        lax.ppermute(cache_packed[k], ZZ, xor_perm(4, k)) for k in range(1, 4)
    ]
    cache_own = jnp.stack(cache_own)

    def around(own):
        return [own] + [lax.ppermute(own, ("yl", "z0"), xor_perm(4, g)) for g in range(1, 4)]

    def sibling(part):
        return lax.ppermute(part, "c", xor_perm(2, 1))

    cache_parts = around(cache_own)

    got = lax.all_to_all(span_packed, ZZ + HEADS, split_axis=0, concat_axis=0, tiled=True)
    queries, span_own = pl.pallas_call(
        unpack_kernel,
        out_shape=(b16(1024, HD), b16(2, 1024, HD)),
        in_specs=[whole()],
        out_specs=(whole(), whole()),
        compiler_params=params(),
        cost_estimate=cost(0, 2 * 2**20),
        name="unpack",
    )(got)
    span_parts = around(span_own)

    biases = pl.pallas_call(
        bias_kernel,
        out_shape=(f32(16, 4096),) + (f32(16, 2048),) * 4,
        in_specs=[scalars(), whole()],
        out_specs=(whole(),) * 5,
        compiler_params=params(),
        cost_estimate=cost(2 * 16 * 192 * 12288, 2**20),
        name="bias",
    )(where, block_mask)

    extra = pl.pallas_call(
        memory_kernel,
        grid_spec=pltpu.PrefetchScalarGridSpec(
            num_scalar_prefetch=1,
            grid=(1,),
            in_specs=[
                scalars(),
                scalars(),
                pl.BlockSpec((1024, HD), lambda i, where: (0, 0)),
                pl.BlockSpec((2, 512, HD), lambda i, where: (0, 0, where[1])),
                pl.BlockSpec((2, 512, HD), lambda i, where: (0, 0, where[1])),
            ],
            out_specs=pl.BlockSpec((1024, HD), lambda i, where: (0, 0)),
        ),
        out_shape=f32(1024, HD),
        compiler_params=params(),
        cost_estimate=cost(4 * 1024 * 1024 * HD, 2**20, 2**20),
        name="memories",
    )(where, mem_lengths, cross_gates, queries, audio_kv, video_kv)

    cache_all = []
    for part in cache_parts:
        cache_all += [part, sibling(part)]
    state = pl.pallas_call(
        cache_kernel,
        out_shape=(f32(1024, HD),) * 3,
        in_specs=[whole()] * 10,
        out_specs=(whole(),) * 3,
        compiler_params=params(),
        cost_estimate=cost(4 * 1024 * 4096 * HD, 4 * 2**20, 4 * 2**20),
        name="cache_attention",
    )(queries, *cache_all, biases[0])

    for g, part in enumerate(span_parts):
        last = g == 3
        operands = [where, queries, part, sibling(part), biases[1 + g], *state]
        if last:
            operands.append(extra)
        state = pl.pallas_call(
            functools.partial(span_kernel, g == 0, last),
            out_shape=b16(4, 256, HD) if last else (f32(1024, HD),) * 3,
            in_specs=[scalars()] + [whole()] * (len(operands) - 1),
            out_specs=whole() if last else (whole(),) * 3,
            compiler_params=params(),
            cost_estimate=cost(4 * 1024 * 1536 * HD, 4 * 2**20, 3 * 2**19),
            name="span_attention",
        )(*operands)

    mixed = [state[0]] + [lax.ppermute(state[k], ZZ, xor_perm(4, k)) for k in range(1, 4)]
    partial_sums = pl.pallas_call(
        project_kernel,
        grid=(4,),
        out_shape=b16(8, 32, 4096),
        in_specs=[scalars()]
        + [pl.BlockSpec((256, HD), lambda i: (0, 0))] * 4
        + [pl.BlockSpec((512, 1024), lambda i: (0, i))],
        out_specs=pl.BlockSpec((8, 32, 1024), lambda i: (0, 0, i)),
        scratch_shapes=[pltpu.VMEM((256, 512), jnp.bfloat16)],
        compiler_params=params(),
        cost_estimate=cost(2 * 256 * 512 * 4096, 6 * 2**20),
        name="project",
    )(where, *mixed, out_weight)
    gathered = lax.all_to_all(partial_sums, HEADS, split_axis=0, concat_axis=0, tiled=True)
    return jnp.sum(gathered.astype(jnp.float32), axis=0).astype(jnp.bfloat16)


def solution(mesh):
    fine = Mesh(mesh.devices.reshape(SIZES), AXES)
    seq = ("yl", "z2", "z1", "z0", "c")
    placed = (
        P(None, seq + HEADS, None),
        P(None, seq, HEADS),
        P(None, None, HEADS),
        P(None, None, HEADS),
        P(HEADS, None, None),
        P(),
        P(None, HEADS),
        P(HEADS, None),
    )
    return jax.shard_map(
        shards, mesh=fine, in_specs=placed, out_specs=P(seq + HEADS, None), check_vma=False
    )
```

```python
import functools
import math

import jax
import jax.numpy as jnp
from jax import lax
from jax.experimental import pallas as pl
from jax.experimental.pallas import tpu as pltpu
from jax.sharding import Mesh
from jax.sharding import PartitionSpec as P

HD = 128
KEYS = 1536
neg_large = -1e30
score_scale = math.log2(math.e) / math.sqrt(HD)

AXES = ("yl", "z2", "z1", "z0", "c", "x", "yh")
SIZES = (2, 2, 2, 2, 2, 4, 2)
ZZ = ("z2", "z1")
HEADS = ("x", "yh")

VM = pltpu.VMEM
SM = pltpu.SMEM
whole = functools.partial(pl.BlockSpec, memory_space=VM)
anywhere = functools.partial(pl.BlockSpec, memory_space=pl.ANY)
scalars = functools.partial(pl.BlockSpec, memory_space=SM)
params = functools.partial(pltpu.CompilerParams, vmem_limit_bytes=40 * 2**20)


def xor_perm(count, k):
    return [(i, i ^ k) for i in range(count)]


def pack_kernel(where_ref, span_ref, cache_ref, span_out, cache_out, sems):
    j = where_ref[1]
    copies = []
    for k in range(4):
        col = pl.multiple_of((j ^ k) * HD, HD)
        copies.append((cache_ref.at[:, :, pl.ds(col, HD)], cache_out.at[k]))
    for d in range(32):
        col = ((d % 8) * 4 + d // 8) * HD
        copies.append((span_ref.at[:, :, pl.ds(col, HD)], span_out.at[d]))
    copies = [
        pltpu.make_async_copy(src, dst, sems.at[n]) for n, (src, dst) in enumerate(copies)
    ]
    for copy in copies:
        copy.start()
    for copy in copies:
        copy.wait()


def unpack_kernel(got_ref, c0_ref, c1_ref, c2_ref, c3_ref, q_out, kv_out):
    for t in range(8):
        first = (t if t < 4 else 7 - t) * 8 + (t // 4) * 4
        rows = slice(t * 128, (t + 1) * 128)
        q_out[rows, :] = got_ref[first:first + 4, 0].reshape(128, HD)
        kv_out[0, rows, :] = got_ref[first:first + 4, 1].reshape(128, HD)
        kv_out[1, rows, :] = got_ref[first:first + 4, 2].reshape(128, HD)
    for k, c_ref in enumerate((c0_ref, c1_ref, c2_ref, c3_ref)):
        kv_out[:, 1024 + k * 128:1024 + (k + 1) * 128, :] = c_ref[...]


def segment_of(t, yl, z0, c):
    low = t < 4
    s = yl * 16 + jnp.where(low, t, 7 - t) * 4 + z0 * 2 + c
    return jnp.where(low, s, 63 - s)


def bias_kernel(where_ref, mask_ref, own_out, near_out):
    yl, j, z0, c = where_ref[0], where_ref[1], where_ref[2], where_ref[3]
    mask = mask_ref[0].astype(jnp.float32).astype(jnp.bfloat16)
    r = lax.broadcasted_iota(jnp.int32, (32, 128), 0)
    qb = 2 * segment_of((r >> 1) & 7, yl, z0 ^ (r >> 4), c) + (r & 1)
    pick = (lax.broadcasted_iota(jnp.int32, (32, 128), 1) == qb).astype(jnp.float32)
    rows = jnp.dot(pick.astype(jnp.bfloat16), mask, preferred_element_type=jnp.float32)
    rows = rows.astype(jnp.bfloat16)

    def spread(block):
        n = block.shape[1]
        one = lax.broadcasted_iota(jnp.int32, (192, n), 0) == jnp.broadcast_to(block, (192, n))
        one = jnp.where(one, 1.0, 0.0).astype(jnp.bfloat16)
        return jnp.dot(rows, one, preferred_element_type=jnp.float32) > 0.5

    for dy, out in enumerate((own_out, near_out)):
        for dc in range(2):
            first = dc * KEYS
            lane = lax.broadcasted_iota(jnp.int32, (1, 1024), 1)
            b = (lane >> 6) & 1
            kb = 2 * segment_of(lane >> 7, yl ^ dy, z0, c ^ dc) + b
            ok = spread(kb + 64).astype(jnp.int32)
            q_full = jnp.broadcast_to(qb[:, :1], (32, 1024))
            k_full = jnp.broadcast_to(kb, (32, 1024))
            ok = ((k_full < q_full) & (ok != 0)) | (k_full == q_full)
            out[:, first:first + 1024] = jnp.where(ok, 0.0, neg_large)
            lane = lax.broadcasted_iota(jnp.int32, (1, 512), 1)
            b = (lane >> 6) & 1
            s = (yl ^ dy) * 16 + (j ^ (lane >> 7)) * 4 + z0 * 2 + (c ^ dc)
            ok = spread(2 * s + b)
            out[:, first + 1024:first + KEYS] = jnp.where(ok, 0.0, neg_large)


def score_tile(q, keys):
    return lax.dot_general(
        q, keys, (((1,), (1,)), ((), ())), preferred_element_type=jnp.float32
    )


def lane_sums(p):
    total = p[:, :HD]
    for i in range(1, p.shape[1] // HD):
        total = total + p[:, i * HD:(i + 1) * HD]
    return total


def fold(state, q, keys, values, bias_ref, block, lanes, causal=None):
    top, total, acc = state
    raw = score_tile(q, keys) * score_scale
    parts = []
    for i in range(q.shape[0] // 64):
        parts.append(raw[i * 64:(i + 1) * 64] + bias_ref[pl.ds(block + i, 1), lanes])
    s = jnp.concatenate(parts, axis=0)
    if causal is not None:
        s = s + causal
    new_top = jnp.maximum(top, jnp.max(s, axis=1, keepdims=True))
    factor = jnp.exp2(top - new_top)
    p = jnp.exp2(s - new_top[:, :1])
    total = total * factor + lane_sums(p)
    acc = acc * factor + jnp.dot(
        p.astype(jnp.bfloat16), values, preferred_element_type=jnp.float32
    )
    return new_top, total, acc


def fresh(rows):
    return (
        jnp.full((rows, HD), neg_large, jnp.float32),
        jnp.zeros((rows, HD), jnp.float32),
        jnp.zeros((rows, HD), jnp.float32),
    )


def fold_range(state, q, kv_ref, bias_ref, block, dc, first, causal=None):
    keys = slice(first, first + 512)
    lanes = slice(dc * KEYS + first, dc * KEYS + first + 512)
    return fold(
        state, q, kv_ref[0, keys, :], kv_ref[1, keys, :], bias_ref, block, lanes, causal
    )


def own_kernel(q0_ref, q1_ref, kv0_ref, kv1_ref, bias_ref, top_out, total_out, acc_out):
    for tile in range(4):
        q_ref = (q0_ref, q1_ref)[tile // 2]
        high = tile % 2
        q = q_ref[high * 512:(high + 1) * 512, :]
        state = fresh(512)
        for dc, kv_ref in enumerate((kv0_ref, kv1_ref)):
            for first in (0, 512, 1024):
                if first == 512 and not high:
                    continue
                causal = None
                if tile < 2 and dc == 0 and first == high * 512:
                    row = lax.broadcasted_iota(jnp.int32, (512, 512), 0)
                    col = lax.broadcasted_iota(jnp.int32, (512, 512), 1)
                    causal = jnp.where(col <= row, 0.0, neg_large)
                state = fold_range(state, q, kv_ref, bias_ref, tile * 8, dc, first, causal)
        rows = slice(tile * 512, (tile + 1) * 512)
        top_out[rows, :], total_out[rows, :], acc_out[rows, :] = state


def near_fold(where_ref, which, q_ref, kv_refs, bias_ref, refs, top, total, acc):
    yl = where_ref[0]
    for high in range(2):
        rows = slice(high * 512, (high + 1) * 512)
        state_rows = slice(which * 1024 + high * 512, which * 1024 + (high + 1) * 512)
        q = q_ref[rows, :]
        block = which * 16 + high * 8
        state = tuple(ref[state_rows, :] for ref in refs)
        for dc, kv_ref in enumerate(kv_refs):
            for first in (0, 1024) if high else (1024,):
                state = fold_range(state, q, kv_ref, bias_ref, block, dc, first)
        top[rows, :], total[rows, :], acc[rows, :] = state

        @pl.when(yl == 1 - high)
        def _():
            state = top[rows, :], total[rows, :], acc[rows, :]
            for dc, kv_ref in enumerate(kv_refs):
                state = fold_range(state, q, kv_ref, bias_ref, block, dc, high * 512)
            top[rows, :], total[rows, :], acc[rows, :] = state


def to_row(column):
    row = lax.broadcasted_iota(jnp.int32, (128, HD), 0)
    col = lax.broadcasted_iota(jnp.int32, (128, HD), 1)
    return jnp.sum(jnp.where(row == col, column, 0.0), axis=0, keepdims=True)


def to_column(line):
    row = lax.broadcasted_iota(jnp.int32, (128, HD), 0)
    col = lax.broadcasted_iota(jnp.int32, (128, HD), 1)
    return jnp.sum(jnp.where(row == col, line, 0.0), axis=1, keepdims=True)


def near_partner_kernel(
    where_ref, q_ref, kv0_ref, kv1_ref, bias_ref, t_ref, l_ref, a_ref, part_out, stats_out,
    top, total, acc,
):
    near_fold(
        where_ref, 1, q_ref, (kv0_ref, kv1_ref), bias_ref, (t_ref, l_ref, a_ref), top, total, acc
    )
    for t in range(8):
        rows = slice(t * 128, (t + 1) * 128)
        weight = jnp.sum(total[rows, :], axis=1, keepdims=True)
        part_out[rows, :] = (acc[rows, :] / weight).astype(jnp.bfloat16)
        stats_out[t:t + 1, :] = to_row(top[rows, :])
        stats_out[8 + t:9 + t, :] = to_row(jnp.broadcast_to(weight, (128, HD)))


def near_own_kernel(
    where_ref, q_ref, kv0_ref, kv1_ref, bias_ref, t_ref, l_ref, a_ref, top, total, acc
):
    near_fold(
        where_ref, 0, q_ref, (kv0_ref, kv1_ref), bias_ref, (t_ref, l_ref, a_ref), top, total, acc
    )


def combine_kernel(where_ref, top, total, acc, part_ref, stats_ref, extra_ref, out_ref):
    j = where_ref[1]
    for t in range(8):
        rows = slice(t * 128, (t + 1) * 128)
        other_top = to_column(stats_ref[t:t + 1, :])
        other_weight = to_column(stats_ref[8 + t:9 + t, :])
        best = jnp.maximum(top[rows, :], other_top)
        factor = jnp.exp2(top[rows, :] - best)
        other = jnp.exp2(other_top - best) * other_weight
        weight = jnp.sum(total[rows, :], axis=1, keepdims=True) * factor + other
        own = acc[rows, :] * factor + part_ref[rows, :].astype(jnp.float32) * other
        mixed = (own / weight + extra_ref[rows, :]).astype(jnp.bfloat16)
        to = t if t < 4 else 7 - t
        half = t // 4
        out_ref[j ^ to, half * 128:(half + 1) * 128, :] = mixed


def memory_kernel(where_ref, len_ref, gate_ref, q_ref, audio_ref, video_ref, out_ref):
    j = where_ref[1]
    slot = lax.broadcasted_iota(jnp.int32, (1, 512), 1)

    def step(w, _):
        rows = pl.ds(pl.multiple_of(w * 512, 512), 512)
        q = q_ref[rows, :]
        mixed = jnp.zeros((512, HD), jnp.float32)
        for n, mem_ref in enumerate((audio_ref, video_ref)):
            bias = jnp.where(slot < len_ref[n], 0.0, neg_large)
            s = score_tile(q, mem_ref[0]) * score_scale + bias
            p = jnp.exp2(s - jnp.max(s, axis=1, keepdims=True))
            total = jnp.sum(p, axis=1, keepdims=True)
            part = jnp.dot(
                p.astype(jnp.bfloat16), mem_ref[1], preferred_element_type=jnp.float32
            )
            gate = jnp.tanh(jnp.full((1, HD), gate_ref[n, j], jnp.float32))
            mixed = mixed + gate * (part / total)
        out_ref[rows, :] = mixed
        return 0

    lax.fori_loop(0, 2, step, 0)


def project_kernel(where_ref, m0, m1, m2, m3, w_ref, out_ref, mixed):
    j = where_ref[1]

    @pl.when(pl.program_id(0) == 0)
    def _():
        for k, m in enumerate((m0, m1, m2, m3)):
            mixed[:, pl.ds(pl.multiple_of((j ^ k) * HD, HD), HD)] = m[...]

    part = jnp.dot(mixed[...], w_ref[...], preferred_element_type=jnp.float32)
    part = part.astype(jnp.bfloat16)
    for h in range(8):
        out_ref[h] = part[h * 32:(h + 1) * 32]


def cost(us):
    return pl.CostEstimate(flops=int(us * 1.15e9), bytes_accessed=2**20, transcendentals=0)


def f32(*shape):
    return jax.ShapeDtypeStruct(shape, jnp.float32)


def b16(*shape):
    return jax.ShapeDtypeStruct(shape, jnp.bfloat16)


def shards(
    span_qkv, cache_kv, audio_kv, video_kv, block_mask, mem_lengths, cross_gates, out_weight
):
    j = lax.axis_index("z2") * 2 + lax.axis_index("z1")
    where = jnp.stack(
        [lax.axis_index("yl"), j, lax.axis_index("z0"), lax.axis_index("c")]
    ).astype(jnp.int32)

    span_packed, cache_packed = pl.pallas_call(
        pack_kernel,
        out_shape=(b16(32, 3, 32, HD), b16(4, 2, 128, HD)),
        in_specs=[scalars(), anywhere(), anywhere()],
        out_specs=(anywhere(), anywhere()),
        scratch_shapes=[pltpu.SemaphoreType.DMA((36,))],
        compiler_params=params(),
        cost_estimate=cost(2),
        name="pack",
    )(where, span_qkv, cache_kv)

    cache_own = [cache_packed[0]] + [
        lax.ppermute(cache_packed[k], ZZ, xor_perm(4, k)) for k in range(1, 4)
    ]
    got = lax.all_to_all(span_packed, ZZ + HEADS, split_axis=0, concat_axis=0, tiled=True)

    def swap(part, axis):
        return lax.ppermute(part, axis, xor_perm(2, 1))

    queries, kv_own = pl.pallas_call(
        unpack_kernel,
        out_shape=(b16(1024, HD), b16(2, KEYS, HD)),
        in_specs=[whole()] * 5,
        out_specs=(whole(), whole()),
        compiler_params=params(),
        cost_estimate=cost(1),
        name="unpack",
    )(got, *cache_own)
    kv_near = swap(kv_own, "yl")
    partner_queries = swap(queries, "z0")
    kv_sibling = swap(kv_own, "c")
    kv_near_sibling = swap(kv_near, "c")

    own_bias, near_bias = pl.pallas_call(
        bias_kernel,
        out_shape=(f32(32, 2 * KEYS),) * 2,
        in_specs=[scalars(), whole()],
        out_specs=(whole(),) * 2,
        compiler_params=params(),
        cost_estimate=cost(2),
        name="bias",
    )(where, block_mask)

    extra = pl.pallas_call(
        memory_kernel,
        grid_spec=pltpu.PrefetchScalarGridSpec(
            num_scalar_prefetch=1,
            grid=(1,),
            in_specs=[
                scalars(),
                scalars(),
                pl.BlockSpec((1024, HD), lambda i, where: (0, 0)),
                pl.BlockSpec((2, 512, HD), lambda i, where: (0, 0, where[1])),
                pl.BlockSpec((2, 512, HD), lambda i, where: (0, 0, where[1])),
            ],
            out_specs=pl.BlockSpec((1024, HD), lambda i, where: (0, 0)),
        ),
        out_shape=f32(1024, HD),
        compiler_params=params(),
        cost_estimate=cost(3),
        name="memories",
    )(where, mem_lengths, cross_gates, queries, audio_kv, video_kv)

    state = pl.pallas_call(
        own_kernel,
        out_shape=(f32(2048, HD),) * 3,
        in_specs=[whole()] * 5,
        out_specs=(whole(),) * 3,
        compiler_params=params(),
        cost_estimate=cost(8),
        name="own_keys",
    )(queries, partner_queries, kv_own, kv_sibling, own_bias)

    part, stats = pl.pallas_call(
        near_partner_kernel,
        out_shape=(b16(1024, HD), f32(16, HD)),
        in_specs=[scalars()] + [whole()] * 7,
        out_specs=(whole(),) * 2,
        scratch_shapes=[pltpu.VMEM((1024, HD), jnp.float32)] * 3,
        compiler_params=params(),
        cost_estimate=cost(4),
        name="near_keys_partner",
    )(where, partner_queries, kv_near, kv_near_sibling, near_bias, *state)
    part = swap(part, "z0")
    stats = swap(stats, "z0")
    state = pl.pallas_call(
        near_own_kernel,
        out_shape=(f32(1024, HD),) * 3,
        in_specs=[scalars()] + [whole()] * 7,
        out_specs=(whole(),) * 3,
        compiler_params=params(),
        cost_estimate=cost(4),
        name="near_keys_own",
    )(where, queries, kv_near, kv_near_sibling, near_bias, *state)
    state = pl.pallas_call(
        combine_kernel,
        out_shape=b16(4, 256, HD),
        in_specs=[scalars()] + [whole()] * 6,
        out_specs=whole(),
        compiler_params=params(),
        cost_estimate=cost(1),
        name="combine",
    )(where, *state, part, stats, extra)

    mixed = [state[0]] + [lax.ppermute(state[k], ZZ, xor_perm(4, k)) for k in range(1, 4)]
    partial_sums = pl.pallas_call(
        project_kernel,
        grid=(4,),
        out_shape=b16(8, 32, 4096),
        in_specs=[scalars()]
        + [pl.BlockSpec((256, HD), lambda i: (0, 0))] * 4
        + [pl.BlockSpec((512, 1024), lambda i: (0, i))],
        out_specs=pl.BlockSpec((8, 32, 1024), lambda i: (0, 0, i)),
        scratch_shapes=[pltpu.VMEM((256, 512), jnp.bfloat16)],
        compiler_params=params(),
        cost_estimate=cost(3),
        name="project",
    )(where, *mixed, out_weight)
    gathered = lax.all_to_all(partial_sums, HEADS, split_axis=0, concat_axis=0, tiled=True)
    return jnp.sum(gathered.astype(jnp.float32), axis=0).astype(jnp.bfloat16)


def solution(mesh):
    fine = Mesh(mesh.devices.reshape(SIZES), AXES)
    seq = ("yl", "z2", "z1", "z0", "c")
    placed = (
        P(None, seq + HEADS, None),
        P(None, seq, HEADS),
        P(None, None, HEADS),
        P(None, None, HEADS),
        P(HEADS, None, None),
        P(),
        P(None, HEADS),
        P(HEADS, None),
    )
    return jax.shard_map(
        shards, mesh=fine, in_specs=placed, out_specs=P(seq + HEADS, None), check_vma=False
    )
```

```python
import functools
import math

import jax
import jax.numpy as jnp
from jax import lax
from jax.experimental import pallas as pl
from jax.experimental.pallas import tpu as pltpu
from jax.sharding import Mesh
from jax.sharding import PartitionSpec as P

HD = 128
KEYS = 1536
neg_large = -1e30
score_scale = math.log2(math.e) / math.sqrt(HD)

AXES = ("yl", "z2", "z1", "z0", "c", "x", "yh")
SIZES = (2, 2, 2, 2, 2, 4, 2)
ZZ = ("z2", "z1")
HEADS = ("x", "yh")

VM = pltpu.VMEM
SM = pltpu.SMEM
whole = functools.partial(pl.BlockSpec, memory_space=VM)
anywhere = functools.partial(pl.BlockSpec, memory_space=pl.ANY)
scalars = functools.partial(pl.BlockSpec, memory_space=SM)


def params(vmem_limit_bytes=24 * 2**20):
    return pltpu.CompilerParams(vmem_limit_bytes=vmem_limit_bytes)


def xor_perm(count, k):
    return [(i, i ^ k) for i in range(count)]


def pack_kernel(where_ref, span_ref, cache_ref, span_out, cache_out):
    j = where_ref[1]
    for k in range(4):
        cache_out[k] = cache_ref[:, :, pl.ds(pl.multiple_of((j ^ k) * HD, HD), HD)]
    for d in range(32):
        col = ((d % 8) * 4 + d // 8) * HD
        span_out[d] = span_ref[:, :, col:col + HD]


def copy_keys(got_ref, cache_refs, kv_out):
    for t in range(8):
        first = (7 - t) * 8 + 4 if t > 3 else t * 8
        rows = slice(t * 128, (t + 1) * 128)
        for n in range(2):
            kv_out[n, rows, :] = got_ref[first:first + 4, 1 + n].reshape(128, HD)
    for k, c_ref in enumerate(cache_refs):
        kv_out[:, 1024 + k * 128:1024 + (k + 1) * 128, :] = c_ref[...]


def unpack_keys_kernel(got_ref, c0_ref, c1_ref, c2_ref, c3_ref, token_ref, kv_out):
    copy_keys(got_ref, (c0_ref, c1_ref, c2_ref, c3_ref), kv_out)


def unpack_rest_kernel(
    got_ref, c0_ref, c1_ref, c2_ref, c3_ref, token_ref, q_out, kv_out
):
    for t in range(8):
        first = (7 - t) * 8 + 4 if t > 3 else t * 8
        q_out[t * 128:(t + 1) * 128, :] = got_ref[first:first + 4, 0].reshape(128, HD)
    copy_keys(got_ref, (c0_ref, c1_ref, c2_ref, c3_ref), kv_out)


def segment_of(t, yl, z0, c):
    low = t < 4
    s = yl * 16 + jnp.where(low, t, 7 - t) * 4 + z0 * 2 + c
    return jnp.where(low, s, 63 - s)


def bias_kernel(where_ref, mask_ref, own_out, near_out):
    yl, j, z0, c = where_ref[0], where_ref[1], where_ref[2], where_ref[3]
    mask = mask_ref[0].astype(jnp.float32).astype(jnp.bfloat16)
    r = lax.broadcasted_iota(jnp.int32, (32, 128), 0)
    qb = 2 * segment_of((r >> 1) & 7, yl, z0 ^ (r >> 4), c) + (r & 1)
    pick = (lax.broadcasted_iota(jnp.int32, (32, 128), 1) == qb).astype(jnp.float32)
    rows = jnp.dot(pick.astype(jnp.bfloat16), mask, preferred_element_type=jnp.float32)
    rows = rows.astype(jnp.bfloat16)

    def spread(block):
        n = block.shape[1]
        one = lax.broadcasted_iota(jnp.int32, (192, n), 0) == jnp.broadcast_to(block, (192, n))
        one = jnp.where(one, 1.0, 0.0).astype(jnp.bfloat16)
        return jnp.dot(rows, one, preferred_element_type=jnp.float32) > 0.5

    def span_bias(dy, dc):
        lane = lax.broadcasted_iota(jnp.int32, (1, 1024), 1)
        kb = 2 * segment_of(lane >> 7, yl ^ dy, z0, c ^ dc) + ((lane >> 6) & 1)
        ok = spread(kb + 64).astype(jnp.int32)
        q_full = jnp.broadcast_to(qb[:, :1], (32, 1024))
        k_full = jnp.broadcast_to(kb, (32, 1024))
        ok = ((k_full < q_full) & (ok != 0)) | (k_full == q_full)
        return jnp.where(ok, 0.0, neg_large)

    def cache_bias(dy, dc):
        lane = lax.broadcasted_iota(jnp.int32, (1, 512), 1)
        s = (yl ^ dy) * 16 + (j ^ (lane >> 7)) * 4 + z0 * 2 + (c ^ dc)
        return jnp.where(spread(2 * s + ((lane >> 6) & 1)), 0.0, neg_large)

    for dy, out in enumerate((own_out, near_out)):
        for dc in range(2):
            out[:, dc * KEYS:dc * KEYS + 1024] = span_bias(dy, dc)
            out[:, dc * KEYS + 1024:(dc + 1) * KEYS] = cache_bias(dy, dc)


def score_tile(q, keys):
    return lax.dot_general(
        q, keys, (((1,), (1,)), ((), ())), preferred_element_type=jnp.float32
    )


def lane_sums(p):
    total = p[:, :HD]
    for i in range(1, p.shape[1] // HD):
        total = total + p[:, i * HD:(i + 1) * HD]
    return total


def attend(state, q, jobs, bias_ref, block):
    def scores(job):
        kv_ref, first = job[:2]
        return score_tile(q, kv_ref[0, first:first + 512, :])

    raws = [scores(jobs[0])]
    for n, (kv_ref, first, lanes, causal) in enumerate(jobs):
        if n + 1 < len(jobs):
            raws.append(scores(jobs[n + 1]))
        raw = raws[n] * score_scale
        parts = []
        for i in range(q.shape[0] // 64):
            bias = bias_ref[block + i:block + i + 1, lanes:lanes + 512]
            parts.append(raw[i * 64:(i + 1) * 64] + bias)
        s = jnp.concatenate(parts, axis=0)
        if causal:
            row = lax.broadcasted_iota(jnp.int32, s.shape, 0)
            col = lax.broadcasted_iota(jnp.int32, s.shape, 1)
            s = jnp.where(col <= row, s, neg_large)
        top, total, acc = state
        new_top = jnp.maximum(top, jnp.max(s, axis=1, keepdims=True))
        factor = jnp.exp2(top - new_top)
        p = jnp.exp2(s - new_top[:, :1])
        total = total * factor + lane_sums(p)
        acc = acc * factor + jnp.dot(
            p.astype(jnp.bfloat16),
            kv_ref[1, first:first + 512, :],
            preferred_element_type=jnp.float32,
        )
        state = new_top, total, acc
    return state


def fresh(rows):
    return (
        jnp.full((rows, HD), neg_large, jnp.float32),
        jnp.zeros((rows, HD), jnp.float32),
        jnp.zeros((rows, HD), jnp.float32),
    )


def own_kernel(which, q_ref, kv0, kv1, bias_ref, top, total, acc):
    for high in range(2):
        jobs = []
        for dc, kv_ref in enumerate((kv0, kv1)):
            lanes = dc * KEYS
            causal = which == 0 and dc == 0
            jobs.append((kv_ref, 1024, lanes + 1024, False))
            jobs.append((kv_ref, 0, lanes, causal and not high))
            if high:
                jobs.append((kv_ref, 512, lanes + 512, causal))
        rows = slice(high * 512, (high + 1) * 512)
        top[rows, :], total[rows, :], acc[rows, :] = attend(
            fresh(512), q_ref[rows, :], jobs, bias_ref, which * 16 + high * 8
        )


def near_fold(yl, which, q_ref, kv_refs, bias_ref, refs, done):
    def variant(firsts):
        for high in range(2):
            rows = slice(high * 512, (high + 1) * 512)
            jobs = [
                (kv_ref, first, dc * KEYS + first, False)
                for dc, kv_ref in kv_refs for first in firsts[high]
            ]
            state = attend(
                tuple(ref[rows, :] for ref in refs), q_ref[rows, :], jobs, bias_ref,
                which * 16 + high * 8,
            )
            done(high, *state)

    @pl.when(yl == 1)
    def _():
        variant(((0, 1024), (0, 1024)))

    @pl.when(yl == 0)
    def _():
        variant(((1024,), (0, 512, 1024)))


def to_row(column):
    row = lax.broadcasted_iota(jnp.int32, (128, HD), 0)
    col = lax.broadcasted_iota(jnp.int32, (128, HD), 1)
    return jnp.sum(jnp.where(row == col, column, 0.0), axis=0, keepdims=True)


def to_column(line):
    row = lax.broadcasted_iota(jnp.int32, (128, HD), 0)
    col = lax.broadcasted_iota(jnp.int32, (128, HD), 1)
    return jnp.sum(jnp.where(row == col, line, 0.0), axis=1, keepdims=True)


def near_partner_kernel(where_ref, q_ref, kv_ref, bias_ref, t_ref, l_ref, a_ref, part_out, levels):
    def done(high, top, total, acc):
        weight = jnp.sum(total, axis=1, keepdims=True)
        part_out[high * 512:(high + 1) * 512, :] = (acc / weight).astype(jnp.bfloat16)
        level = top + jnp.log2(jnp.broadcast_to(weight, (512, HD)))
        for i in range(4):
            t = high * 4 + i
            levels[t:t + 1, :] = to_row(level[i * 128:(i + 1) * 128])

    near_fold(
        where_ref[0], 1, q_ref, ((1, kv_ref),), bias_ref, (t_ref, l_ref, a_ref), done
    )
    rest = levels[...]
    pieces = []
    for _ in range(4):
        piece = rest.astype(jnp.bfloat16).astype(jnp.float32)
        rest = rest - piece
        pieces.append(piece)
    part_out[1024:, :] = jnp.concatenate(pieces, axis=0).astype(jnp.bfloat16)


def near_kernel(which, cores, where_ref, q_ref, *refs):
    def done(high, *state):
        rows = slice(high * 512, (high + 1) * 512)
        for ref, value in zip(refs[-3:], state):
            ref[rows, :] = value

    kv_refs = tuple(zip(cores, refs))
    refs = refs[len(cores):]
    near_fold(where_ref[0], which, q_ref, kv_refs, refs[0], refs[1:4], done)


def combine_kernel(where_ref, top, total, acc, part_ref, extra_ref, out_ref):
    j = where_ref[1]
    pieces = part_ref[1024:, :].astype(jnp.float32)
    levels = pieces[0:8] + (pieces[8:16] + (pieces[16:24] + pieces[24:32]))
    for t in range(8):
        rows = slice(t * 128, (t + 1) * 128)
        level = to_column(levels[t:t + 1])
        best = jnp.maximum(top[rows, :], level)
        factor = jnp.exp2(top[rows, :] - best)
        other = jnp.exp2(level - best)
        weight = jnp.sum(total[rows, :], axis=1, keepdims=True) * factor + other
        own = acc[rows, :] * factor + part_ref[rows, :].astype(jnp.float32) * other
        mixed = (own / weight + extra_ref[rows, :]).astype(jnp.bfloat16)
        to = t if t < 4 else 7 - t
        half = t // 4
        out_ref[j ^ to, half * 128:(half + 1) * 128, :] = mixed


def memory_kernel(where_ref, len_ref, gate_ref, q_ref, audio_ref, video_ref, out_ref):
    j = where_ref[1]
    slot = lax.broadcasted_iota(jnp.int32, (1, 512), 1)
    for high in range(2):
        q = q_ref[high * 512:(high + 1) * 512, :]
        mixed = jnp.zeros((512, HD), jnp.float32)
        raws = [score_tile(q, mem_ref[0]) for mem_ref in (audio_ref, video_ref)]
        for n, mem_ref in enumerate((audio_ref, video_ref)):
            bias = jnp.where(slot < len_ref[n], 0.0, neg_large)
            s = raws[n] * score_scale + bias
            p = jnp.exp2(s - jnp.max(s, axis=1, keepdims=True))
            total = jnp.sum(lane_sums(p), axis=1, keepdims=True)
            part = jnp.dot(
                p.astype(jnp.bfloat16), mem_ref[1], preferred_element_type=jnp.float32
            )
            gate = jnp.tanh(jnp.full((1, HD), gate_ref[n, j], jnp.float32))
            mixed = mixed + gate * (part / total)
        out_ref[high * 512:(high + 1) * 512, :] = mixed


def project_kernel(where_ref, m0, m1, m2, m3, w_ref, out_ref, mixed):
    j = where_ref[1]

    @pl.when(pl.program_id(0) == 0)
    def _():
        for k, m in enumerate((m0, m1, m2, m3)):
            mixed[:, pl.ds(pl.multiple_of((j ^ k) * HD, HD), HD)] = m[...]

    part = jnp.dot(mixed[...], w_ref[...], preferred_element_type=jnp.float32)
    part = part.astype(jnp.bfloat16)
    for h in range(8):
        out_ref[h] = part[h * 32:(h + 1) * 32]


def cost(us):
    return pl.CostEstimate(flops=int(us * 1.15e9), bytes_accessed=2**20, transcendentals=0)


def after(array, token):
    def kernel(array_ref, token_ref, out_ref):
        pass

    return pl.pallas_call(
        kernel,
        out_shape=jax.ShapeDtypeStruct(array.shape, array.dtype),
        in_specs=[anywhere(), anywhere()],
        out_specs=anywhere(),
        input_output_aliases={0: 0},
        compiler_params=params(),
        name="after",
    )(array, token)


def f32(*shape):
    return jax.ShapeDtypeStruct(shape, jnp.float32)


def b16(*shape):
    return jax.ShapeDtypeStruct(shape, jnp.bfloat16)


def shards(
    span_qkv, cache_kv, audio_kv, video_kv, block_mask, mem_lengths, cross_gates, out_weight
):
    j = lax.axis_index("z2") * 2 + lax.axis_index("z1")
    where = jnp.stack(
        [lax.axis_index("yl"), j, lax.axis_index("z0"), lax.axis_index("c")]
    ).astype(jnp.int32)

    span_packed, cache_packed = pl.pallas_call(
        pack_kernel,
        out_shape=(b16(32, 3, 32, HD), b16(4, 2, 128, HD)),
        in_specs=[scalars(), whole(), whole()],
        out_specs=(whole(),) * 2,
        compiler_params=params(),
        cost_estimate=cost(2),
        name="pack",
    )(where, span_qkv, cache_kv)

    def swap(part, axis):
        return lax.ppermute(part, axis, xor_perm(2, 1))

    def swap_z(parts):
        return [parts[0]] + [lax.ppermute(parts[k], ZZ, xor_perm(4, k)) for k in range(1, 4)]

    own_bias, near_bias = pl.pallas_call(
        bias_kernel,
        out_shape=(f32(32, 2 * KEYS),) * 2,
        in_specs=[scalars(), whole()],
        out_specs=(whole(),) * 2,
        compiler_params=params(),
        cost_estimate=cost(2),
        name="bias",
    )(where, block_mask)

    got = lax.all_to_all(span_packed, ZZ + HEADS, split_axis=0, concat_axis=0, tiled=True)
    cache_own = swap_z([cache_packed[k] for k in range(4)])
    def unpack(kernel, token, name, *outs):
        return pl.pallas_call(
            kernel,
            out_shape=outs,
            in_specs=[whole()] * 5 + [anywhere()],
            out_specs=(whole(),) * len(outs),
            compiler_params=params(),
            cost_estimate=cost(0.1),
            name=name,
        )(got, *cache_own, token)

    (kv_sent,) = unpack(unpack_keys_kernel, own_bias, "unpack_keys", b16(2, KEYS, HD))
    kv_near = swap(kv_sent, "yl")
    queries, kv_own = unpack(
        unpack_rest_kernel, kv_sent, "unpack_rest", b16(1024, HD), b16(2, KEYS, HD)
    )
    partner_queries = swap(queries, "z0")
    sibling_keys = swap(kv_own, "c")

    extra = pl.pallas_call(
        memory_kernel,
        grid_spec=pltpu.PrefetchScalarGridSpec(
            num_scalar_prefetch=1,
            grid=(1,),
            in_specs=[
                scalars(),
                scalars(),
                pl.BlockSpec((1024, HD), lambda i, where: (0, 0)),
                pl.BlockSpec((2, 512, HD), lambda i, where: (0, 0, where[1])),
                pl.BlockSpec((2, 512, HD), lambda i, where: (0, 0, where[1])),
            ],
            out_specs=pl.BlockSpec((1024, HD), lambda i, where: (0, 0)),
        ),
        out_shape=f32(1024, HD),
        compiler_params=params(),
        cost_estimate=cost(0.1),
        name="memories",
    )(where, mem_lengths, cross_gates, queries, audio_kv, video_kv)

    def own(which, q):
        return pl.pallas_call(
            functools.partial(own_kernel, which),
            out_shape=(f32(1024, HD),) * 3,
            in_specs=[whole()] * 4,
            out_specs=(whole(),) * 3,
            compiler_params=params(),
            cost_estimate=cost(0.1),
            name="own_keys",
        )(q, kv_own, sibling_keys, own_bias)

    sibling_keys = after(sibling_keys, extra)
    states = [own(0, queries)]
    partner_queries = after(partner_queries, states[0][0])
    states.append(own(1, partner_queries))
    kv_near = after(kv_near, states[1][0])
    near_sibling = swap(kv_near, "c")

    def near(which, cores, q, keys, state):
        return pl.pallas_call(
            functools.partial(near_kernel, which, cores),
            out_shape=(f32(1024, HD),) * 3,
            in_specs=[scalars()] + [whole()] * (5 + len(cores)),
            out_specs=(whole(),) * 3,
            compiler_params=params(),
            cost_estimate=cost(2.5 * len(cores)),
            name="near_keys",
        )(where, q, *keys, near_bias, *state)

    state = near(1, (0,), partner_queries, (kv_near,), states[1])
    part = pl.pallas_call(
        near_partner_kernel,
        out_shape=b16(1056, HD),
        in_specs=[scalars()] + [whole()] * 6,
        out_specs=whole(),
        scratch_shapes=[pltpu.VMEM((8, HD), jnp.float32)],
        compiler_params=params(),
        cost_estimate=cost(3),
        name="near_keys_partner",
    )(where, partner_queries, near_sibling, near_bias, *state)
    part = swap(part, "z0")
    state = near(0, (0, 1), queries, (kv_near, near_sibling), states[0])
    state = pl.pallas_call(
        combine_kernel,
        out_shape=b16(4, 256, HD),
        in_specs=[scalars()] + [whole()] * 5,
        out_specs=whole(),
        compiler_params=params(),
        cost_estimate=cost(1),
        name="combine",
    )(where, *state, part, extra)

    mixed = [state[0]] + [lax.ppermute(state[k], ZZ, xor_perm(4, k)) for k in range(1, 4)]
    partial_sums = pl.pallas_call(
        project_kernel,
        grid=(4,),
        out_shape=b16(8, 32, 4096),
        in_specs=[scalars()]
        + [pl.BlockSpec((256, HD), lambda i: (0, 0))] * 4
        + [pl.BlockSpec((512, 1024), lambda i: (0, i))],
        out_specs=pl.BlockSpec((8, 32, 1024), lambda i: (0, 0, i)),
        scratch_shapes=[pltpu.VMEM((256, 512), jnp.bfloat16)],
        compiler_params=params(),
        cost_estimate=cost(3),
        name="project",
    )(where, *mixed, out_weight)
    gathered = lax.all_to_all(partial_sums, HEADS, split_axis=0, concat_axis=0, tiled=True)
    return jnp.sum(gathered.astype(jnp.float32), axis=0).astype(jnp.bfloat16)


def solution(mesh):
    fine = Mesh(mesh.devices.reshape(SIZES), AXES)
    seq = ("yl", "z2", "z1", "z0", "c")
    placed = (
        P(None, seq + HEADS, None),
        P(None, seq, HEADS),
        P(None, None, HEADS),
        P(None, None, HEADS),
        P(HEADS, None, None),
        P(),
        P(None, HEADS),
        P(HEADS, None),
    )
    return jax.shard_map(
        shards, mesh=fine, in_specs=placed, out_specs=P(seq + HEADS, None), check_vma=False
    )
```

```python
import functools
import math

import jax
import jax.numpy as jnp
from jax import lax
from jax.experimental import pallas as pl
from jax.experimental.pallas import tpu as pltpu
from jax.sharding import Mesh
from jax.sharding import PartitionSpec as P

HD = 128
KEYS = 1536
neg_large = -1e30
score_scale = math.log2(math.e) / math.sqrt(HD)

AXES = ("yl", "z2", "z1", "z0", "c", "x", "yh")
SIZES = (2, 2, 2, 2, 2, 4, 2)
ZZ = ("z2", "z1")
HEADS = ("x", "yh")

VM = pltpu.VMEM
SM = pltpu.SMEM
whole = functools.partial(pl.BlockSpec, memory_space=VM)
anywhere = functools.partial(pl.BlockSpec, memory_space=pl.ANY)
scalars = functools.partial(pl.BlockSpec, memory_space=SM)


def params(vmem_limit_bytes=24 * 2**20):
    return pltpu.CompilerParams(vmem_limit_bytes=vmem_limit_bytes)


def xor_perm(count, k):
    return [(i, i ^ k) for i in range(count)]


def turn_perm(count, k):
    return [(i, (i + k) % count) for i in range(count)]


def pack_kernel(span_ref, span_out):
    for d in range(32):
        col = ((d % 8) * 4 + d // 8) * HD
        span_out[d, 0] = span_ref[0, :, col:col + HD]


def pack_cache_kernel(where_ref, cache_ref, token_ref, cache_out):
    j = where_ref[1]
    for k in range(4):
        cache_out[k] = cache_ref[:, :, pl.ds(pl.multiple_of(((j + k) & 3) * HD, HD), HD)]


def copy_keys(got_ref, cache_refs, kv_out):
    for t in range(8):
        first = (7 - t) * 8 + 4 if t > 3 else t * 8
        rows = slice(t * 128, (t + 1) * 128)
        for n in range(2):
            kv_out[n, rows, :] = got_ref[first:first + 4, 1 + n].reshape(128, HD)
    for k, c_ref in enumerate(cache_refs):
        kv_out[:, 1024 + k * 128:1024 + (k + 1) * 128, :] = c_ref[...]


def unpack_keys_kernel(got_ref, c0_ref, c1_ref, c2_ref, c3_ref, token_ref, kv_out):
    copy_keys(got_ref, (c0_ref, c1_ref, c2_ref, c3_ref), kv_out)


def unpack_rest_kernel(
    got_ref, c0_ref, c1_ref, c2_ref, c3_ref, token_ref, q_out, kv_out
):
    for t in range(8):
        first = (7 - t) * 8 + 4 if t > 3 else t * 8
        q_out[t * 128:(t + 1) * 128, :] = got_ref[first:first + 4, 0].reshape(128, HD)
    copy_keys(got_ref, (c0_ref, c1_ref, c2_ref, c3_ref), kv_out)


def segment_of(t, yl, z0, c):
    low = t < 4
    s = yl * 16 + jnp.where(low, t, 7 - t) * 4 + z0 * 2 + c
    return jnp.where(low, s, 63 - s)


def bias_kernel(where_ref, mask_ref, own_out, near_out):
    yl, j, z0, c = where_ref[0], where_ref[1], where_ref[2], where_ref[3]
    mask = mask_ref[0].astype(jnp.float32).astype(jnp.bfloat16)
    r = lax.broadcasted_iota(jnp.int32, (32, 128), 0)
    qb = 2 * segment_of((r >> 1) & 7, yl, z0 ^ (r >> 4), c) + (r & 1)
    pick = (lax.broadcasted_iota(jnp.int32, (32, 128), 1) == qb).astype(jnp.float32)
    rows = jnp.dot(pick.astype(jnp.bfloat16), mask, preferred_element_type=jnp.float32)
    rows = rows.astype(jnp.bfloat16)

    def spread(block):
        n = block.shape[1]
        one = lax.broadcasted_iota(jnp.int32, (192, n), 0) == jnp.broadcast_to(block, (192, n))
        one = jnp.where(one, 1.0, 0.0).astype(jnp.bfloat16)
        return jnp.dot(rows, one, preferred_element_type=jnp.float32) > 0.5

    def span_bias(dy, dc):
        lane = lax.broadcasted_iota(jnp.int32, (1, 1024), 1)
        kb = 2 * segment_of(lane >> 7, yl ^ dy, z0, c ^ dc) + ((lane >> 6) & 1)
        ok = spread(kb + 64).astype(jnp.int32)
        q_full = jnp.broadcast_to(qb[:, :1], (32, 1024))
        k_full = jnp.broadcast_to(kb, (32, 1024))
        ok = ((k_full < q_full) & (ok != 0)) | (k_full == q_full)
        return jnp.where(ok, 0.0, neg_large)

    def cache_bias(dy, dc):
        lane = lax.broadcasted_iota(jnp.int32, (1, 512), 1)
        s = (yl ^ dy) * 16 + ((j - (lane >> 7)) & 3) * 4 + z0 * 2 + (c ^ dc)
        return jnp.where(spread(2 * s + ((lane >> 6) & 1)), 0.0, neg_large)

    for dy, out in enumerate((own_out, near_out)):
        for dc in range(2):
            out[:, dc * KEYS:dc * KEYS + 1024] = span_bias(dy, dc)
            out[:, dc * KEYS + 1024:(dc + 1) * KEYS] = cache_bias(dy, dc)


def score_tile(q, keys):
    return lax.dot_general(
        q, keys, (((1,), (1,)), ((), ())), preferred_element_type=jnp.float32
    )


def lane_sums(p):
    total = p[:, :HD]
    for i in range(1, p.shape[1] // HD):
        total = total + p[:, i * HD:(i + 1) * HD]
    return total


def attend(state, q, jobs, bias_ref, block):
    def scores(job):
        kv_ref, first = job[:2]
        return score_tile(q, kv_ref[0, first:first + 512, :])

    raws = [scores(jobs[0])]
    for n, (kv_ref, first, lanes, causal) in enumerate(jobs):
        if n + 1 < len(jobs):
            raws.append(scores(jobs[n + 1]))
        raw = raws[n] * score_scale
        parts = []
        for i in range(q.shape[0] // 64):
            bias = bias_ref[block + i:block + i + 1, lanes:lanes + 512]
            parts.append(raw[i * 64:(i + 1) * 64] + bias)
        s = jnp.concatenate(parts, axis=0)
        if causal:
            row = lax.broadcasted_iota(jnp.int32, s.shape, 0)
            col = lax.broadcasted_iota(jnp.int32, s.shape, 1)
            s = jnp.where(col <= row, s, neg_large)
        top, total, acc = state
        new_top = jnp.maximum(top, jnp.max(s, axis=1, keepdims=True))
        factor = jnp.exp2(top - new_top)
        p = jnp.exp2(s - new_top[:, :1])
        total = total * factor + lane_sums(p)
        acc = acc * factor + jnp.dot(
            p.astype(jnp.bfloat16),
            kv_ref[1, first:first + 512, :],
            preferred_element_type=jnp.float32,
        )
        state = new_top, total, acc
    return state


def fresh(rows):
    return (
        jnp.full((rows, HD), neg_large, jnp.float32),
        jnp.zeros((rows, HD), jnp.float32),
        jnp.zeros((rows, HD), jnp.float32),
    )


def own_kernel(which, q_ref, kv0, kv1, bias_ref, top, total, acc):
    for high in range(2):
        jobs = []
        for dc, kv_ref in enumerate((kv0, kv1)):
            lanes = dc * KEYS
            causal = which == 0 and dc == 0
            jobs.append((kv_ref, 1024, lanes + 1024, False))
            jobs.append((kv_ref, 0, lanes, causal and not high))
            if high:
                jobs.append((kv_ref, 512, lanes + 512, causal))
        rows = slice(high * 512, (high + 1) * 512)
        top[rows, :], total[rows, :], acc[rows, :] = attend(
            fresh(512), q_ref[rows, :], jobs, bias_ref, which * 16 + high * 8
        )


def near_fold(yl, which, q_ref, kv_refs, bias_ref, refs, done):
    def variant(firsts):
        for high in range(2):
            rows = slice(high * 512, (high + 1) * 512)
            jobs = [
                (kv_ref, first, dc * KEYS + first, False)
                for dc, kv_ref in kv_refs for first in firsts[high]
            ]
            state = attend(
                tuple(ref[rows, :] for ref in refs), q_ref[rows, :], jobs, bias_ref,
                which * 16 + high * 8,
            )
            done(high, *state)

    @pl.when(yl == 1)
    def _():
        variant(((0, 1024), (0, 1024)))

    @pl.when(yl == 0)
    def _():
        variant(((1024,), (0, 512, 1024)))


def to_row(column):
    row = lax.broadcasted_iota(jnp.int32, (128, HD), 0)
    col = lax.broadcasted_iota(jnp.int32, (128, HD), 1)
    return jnp.sum(jnp.where(row == col, column, 0.0), axis=0, keepdims=True)


def to_column(line):
    row = lax.broadcasted_iota(jnp.int32, (128, HD), 0)
    col = lax.broadcasted_iota(jnp.int32, (128, HD), 1)
    return jnp.sum(jnp.where(row == col, line, 0.0), axis=1, keepdims=True)


def near_partner_kernel(where_ref, q_ref, kv_ref, bias_ref, t_ref, l_ref, a_ref, part_out, levels):
    def done(high, top, total, acc):
        weight = jnp.sum(total, axis=1, keepdims=True)
        part_out[high * 512:(high + 1) * 512, :] = (acc / weight).astype(jnp.bfloat16)
        level = top + jnp.log2(jnp.broadcast_to(weight, (512, HD)))
        for i in range(4):
            t = high * 4 + i
            levels[t:t + 1, :] = to_row(level[i * 128:(i + 1) * 128])

    near_fold(
        where_ref[0], 1, q_ref, ((1, kv_ref),), bias_ref, (t_ref, l_ref, a_ref), done
    )
    rest = levels[...]
    pieces = []
    for _ in range(4):
        piece = rest.astype(jnp.bfloat16).astype(jnp.float32)
        rest = rest - piece
        pieces.append(piece)
    part_out[1024:, :] = jnp.concatenate(pieces, axis=0).astype(jnp.bfloat16)


def near_kernel(which, cores, where_ref, q_ref, *refs):
    def done(high, *state):
        rows = slice(high * 512, (high + 1) * 512)
        for ref, value in zip(refs[-3:], state):
            ref[rows, :] = value

    kv_refs = tuple(zip(cores, refs))
    refs = refs[len(cores):]
    near_fold(where_ref[0], which, q_ref, kv_refs, refs[0], refs[1:4], done)


def combine_kernel(top, total, acc, part_ref, extra_ref, out_ref):
    pieces = part_ref[1024:, :].astype(jnp.float32)
    levels = pieces[0:8] + (pieces[8:16] + (pieces[16:24] + pieces[24:32]))
    for t in range(8):
        rows = slice(t * 128, (t + 1) * 128)
        level = to_column(levels[t:t + 1])
        best = jnp.maximum(top[rows, :], level)
        factor = jnp.exp2(top[rows, :] - best)
        other = jnp.exp2(level - best)
        weight = jnp.sum(total[rows, :], axis=1, keepdims=True) * factor + other
        own = acc[rows, :] * factor + part_ref[rows, :].astype(jnp.float32) * other
        mixed = (own / weight + extra_ref[rows, :]).astype(jnp.bfloat16)
        to = t if t < 4 else 7 - t
        half = t // 4
        out_ref[to, half * 128:(half + 1) * 128, :] = mixed


def memory_kernel(where_ref, len_ref, gate_ref, q_ref, audio_ref, video_ref, out_ref):
    j = where_ref[1]
    slot = lax.broadcasted_iota(jnp.int32, (1, 512), 1)
    for high in range(2):
        q = q_ref[high * 512:(high + 1) * 512, :]
        mixed = jnp.zeros((512, HD), jnp.float32)
        raws = [score_tile(q, mem_ref[0]) for mem_ref in (audio_ref, video_ref)]
        for n, mem_ref in enumerate((audio_ref, video_ref)):
            bias = jnp.where(slot < len_ref[n], 0.0, neg_large)
            s = raws[n] * score_scale + bias
            p = jnp.exp2(s - jnp.max(s, axis=1, keepdims=True))
            total = jnp.sum(lane_sums(p), axis=1, keepdims=True)
            part = jnp.dot(
                p.astype(jnp.bfloat16), mem_ref[1], preferred_element_type=jnp.float32
            )
            gate = jnp.tanh(jnp.full((1, HD), gate_ref[n, j], jnp.float32))
            mixed = mixed + gate * (part / total)
        out_ref[high * 512:(high + 1) * 512, :] = mixed


def project_kernel(got_ref, w_ref, out_ref, mixed):
    @pl.when(pl.program_id(0) == 0)
    def _():
        for j in range(4):
            mixed[:, j * HD:(j + 1) * HD] = got_ref[j]

    part = jnp.dot(mixed[...], w_ref[...], preferred_element_type=jnp.float32)
    part = part.astype(jnp.bfloat16)
    for h in range(8):
        out_ref[h] = part[h * 32:(h + 1) * 32]


def cost(us):
    return pl.CostEstimate(flops=int(us * 1.15e9), bytes_accessed=1024, transcendentals=0)


def after(array, token):
    def kernel(array_ref, token_ref, out_ref):
        pass

    return pl.pallas_call(
        kernel,
        out_shape=jax.ShapeDtypeStruct(array.shape, array.dtype),
        in_specs=[anywhere(), anywhere()],
        out_specs=anywhere(),
        input_output_aliases={0: 0},
        compiler_params=params(),
        cost_estimate=cost(0.001),
        name="after",
    )(array, token)


def f32(*shape):
    return jax.ShapeDtypeStruct(shape, jnp.float32)


def b16(*shape):
    return jax.ShapeDtypeStruct(shape, jnp.bfloat16)


def shards(
    span_qkv, cache_kv, audio_kv, video_kv, block_mask, mem_lengths, cross_gates, out_weight
):
    j = lax.axis_index("z2") * 2 + lax.axis_index("z1")
    where = jnp.stack(
        [lax.axis_index("yl"), j, lax.axis_index("z0"), lax.axis_index("c")]
    ).astype(jnp.int32)

    span_packed = pl.pallas_call(
        pack_kernel,
        grid=(3,),
        out_shape=b16(32, 3, 32, HD),
        in_specs=[pl.BlockSpec((1, 32, 4096), lambda n: (n, 0, 0))],
        out_specs=pl.BlockSpec((32, 1, 32, HD), lambda n: (0, n, 0, 0)),
        compiler_params=params(60 * 2**20),
        cost_estimate=cost(2),
        name="pack",
    )(span_qkv)
    cache_packed = pl.pallas_call(
        pack_cache_kernel,
        out_shape=b16(4, 2, 128, HD),
        in_specs=[scalars(), whole(), anywhere()],
        out_specs=whole(),
        compiler_params=params(),
        cost_estimate=cost(1),
        name="pack_cache",
    )(where, cache_kv, span_packed)

    def swap(part, axis):
        return lax.ppermute(part, axis, xor_perm(2, 1))

    def swap_z(parts):
        return [parts[0]] + [lax.ppermute(parts[k], ZZ, turn_perm(4, k)) for k in range(1, 4)]

    own_bias, near_bias = pl.pallas_call(
        bias_kernel,
        out_shape=(f32(32, 2 * KEYS),) * 2,
        in_specs=[scalars(), whole()],
        out_specs=(whole(),) * 2,
        compiler_params=params(),
        cost_estimate=cost(2),
        name="bias",
    )(where, block_mask)

    got = lax.all_to_all(span_packed, ZZ + HEADS, split_axis=0, concat_axis=0, tiled=True)
    cache_own = swap_z([cache_packed[k] for k in range(4)])
    def unpack(kernel, token, name, *outs):
        return pl.pallas_call(
            kernel,
            out_shape=outs,
            in_specs=[whole()] * 5 + [anywhere()],
            out_specs=(whole(),) * len(outs),
            compiler_params=params(),
            cost_estimate=cost(0.001),
            name=name,
        )(got, *cache_own, token)

    (kv_sent,) = unpack(unpack_keys_kernel, own_bias, "unpack_keys", b16(2, KEYS, HD))
    kv_near = swap(kv_sent, "yl")
    queries, kv_own = unpack(
        unpack_rest_kernel, kv_sent, "unpack_rest", b16(1024, HD), b16(2, KEYS, HD)
    )
    partner_queries = swap(queries, "z0")
    sibling_keys = swap(kv_own, "c")

    extra = pl.pallas_call(
        memory_kernel,
        grid_spec=pltpu.PrefetchScalarGridSpec(
            num_scalar_prefetch=1,
            grid=(1,),
            in_specs=[
                scalars(),
                scalars(),
                pl.BlockSpec((1024, HD), lambda i, where: (0, 0)),
                pl.BlockSpec((2, 512, HD), lambda i, where: (0, 0, where[1])),
                pl.BlockSpec((2, 512, HD), lambda i, where: (0, 0, where[1])),
            ],
            out_specs=pl.BlockSpec((1024, HD), lambda i, where: (0, 0)),
        ),
        out_shape=f32(1024, HD),
        compiler_params=params(),
        cost_estimate=cost(0.001),
        name="memories",
    )(where, mem_lengths, cross_gates, queries, audio_kv, video_kv)

    def own(which, q):
        return pl.pallas_call(
            functools.partial(own_kernel, which),
            out_shape=(f32(1024, HD),) * 3,
            in_specs=[whole()] * 4,
            out_specs=(whole(),) * 3,
            compiler_params=params(),
            cost_estimate=cost(0.001),
            name="own_keys",
        )(q, kv_own, sibling_keys, own_bias)

    sibling_keys = after(sibling_keys, extra)
    states = [own(0, queries)]
    partner_queries = after(partner_queries, states[0][0])
    states.append(own(1, partner_queries))
    kv_near = after(kv_near, states[1][0])
    near_sibling = swap(kv_near, "c")

    def near(which, cores, q, keys, state):
        return pl.pallas_call(
            functools.partial(near_kernel, which, cores),
            out_shape=(f32(1024, HD),) * 3,
            in_specs=[scalars()] + [whole()] * (5 + len(cores)),
            out_specs=(whole(),) * 3,
            compiler_params=params(),
            cost_estimate=cost(2.5 * len(cores)),
            name="near_keys",
        )(where, q, *keys, near_bias, *state)

    state = near(1, (0,), partner_queries, (kv_near,), states[1])
    part = pl.pallas_call(
        near_partner_kernel,
        out_shape=b16(1056, HD),
        in_specs=[scalars()] + [whole()] * 6,
        out_specs=whole(),
        scratch_shapes=[pltpu.VMEM((8, HD), jnp.float32)],
        compiler_params=params(),
        cost_estimate=cost(3),
        name="near_keys_partner",
    )(where, partner_queries, near_sibling, near_bias, *state)
    part = swap(part, "z0")
    state = near(0, (0, 1), queries, (kv_near, near_sibling), states[0])
    state = pl.pallas_call(
        combine_kernel,
        out_shape=b16(4, 256, HD),
        in_specs=[whole()] * 5,
        out_specs=whole(),
        compiler_params=params(),
        cost_estimate=cost(1),
        name="combine",
    )(*state, part, extra)

    mixed = lax.all_to_all(state, ZZ, split_axis=0, concat_axis=0, tiled=True)
    partial_sums = pl.pallas_call(
        project_kernel,
        grid=(4,),
        out_shape=b16(8, 32, 4096),
        in_specs=[
            pl.BlockSpec((4, 256, HD), lambda i: (0, 0, 0)),
            pl.BlockSpec((512, 1024), lambda i: (0, i)),
        ],
        out_specs=pl.BlockSpec((8, 32, 1024), lambda i: (0, 0, i)),
        scratch_shapes=[pltpu.VMEM((256, 512), jnp.bfloat16)],
        compiler_params=params(),
        cost_estimate=cost(3),
        name="project",
    )(mixed, out_weight)
    gathered = lax.all_to_all(partial_sums, HEADS, split_axis=0, concat_axis=0, tiled=True)
    return jnp.sum(gathered.astype(jnp.float32), axis=0).astype(jnp.bfloat16)


def solution(mesh):
    fine = Mesh(mesh.devices.reshape(SIZES), AXES)
    seq = ("yl", "z2", "z1", "z0", "c")
    placed = (
        P(None, seq + HEADS, None),
        P(None, seq, HEADS),
        P(None, None, HEADS),
        P(None, None, HEADS),
        P(HEADS, None, None),
        P(),
        P(None, HEADS),
        P(HEADS, None),
    )
    return jax.shard_map(
        shards, mesh=fine, in_specs=placed, out_specs=P(seq + HEADS, None), check_vma=False
    )
```

```python
import functools
import math

import jax
import jax.numpy as jnp
from jax import lax
from jax.experimental import pallas as pl
from jax.experimental.pallas import tpu as pltpu
from jax.sharding import Mesh
from jax.sharding import PartitionSpec as P

HD = 128
KEYS = 1536
neg_large = -1e30
score_scale = math.log2(math.e) / math.sqrt(HD)

AXES = ("yl", "z2", "z1", "z0", "c", "x", "yh")
SIZES = (2, 2, 2, 2, 2, 4, 2)
ZZ = ("z2", "z1")
HEADS = ("x", "yh")

VM = pltpu.VMEM
SM = pltpu.SMEM
whole = functools.partial(pl.BlockSpec, memory_space=VM)
anywhere = functools.partial(pl.BlockSpec, memory_space=pl.ANY)
scalars = functools.partial(pl.BlockSpec, memory_space=SM)


def params(vmem_limit_bytes=24 * 2**20):
    return pltpu.CompilerParams(vmem_limit_bytes=vmem_limit_bytes)


def xor_perm(count, k):
    return [(i, i ^ k) for i in range(count)]


def turn_perm(count, k):
    return [(i, (i + k) % count) for i in range(count)]


def pack_kernel(span_ref, span_out, span_in, packed, sems):
    reads = [
        pltpu.make_async_copy(span_ref.at[n], span_in.at[n], sems.at[n]) for n in range(3)
    ]
    for copy in reads:
        copy.start()
    for n in range(3):
        reads[n].wait()
        for d in range(32):
            col = ((d % 8) * 4 + d // 8) * HD
            packed[d, n] = span_in[n, :, col:col + HD]
    write = pltpu.make_async_copy(packed, span_out, sems.at[3])
    write.start()
    write.wait()


def pack_cache_kernel(where_ref, cache_ref, token_ref, cache_out):
    j = where_ref[1]
    for k in range(4):
        cache_out[k] = cache_ref[:, :, pl.ds(pl.multiple_of(((j + k) & 3) * HD, HD), HD)]


def copy_keys(got_ref, cache_refs, kv_out):
    for t in range(8):
        first = (7 - t) * 8 + 4 if t > 3 else t * 8
        rows = slice(t * 128, (t + 1) * 128)
        for n in range(2):
            kv_out[n, rows, :] = got_ref[first:first + 4, 1 + n].reshape(128, HD)
    for k, c_ref in enumerate(cache_refs):
        kv_out[:, 1024 + k * 128:1024 + (k + 1) * 128, :] = c_ref[...]


def unpack_keys_kernel(got_ref, c0_ref, c1_ref, c2_ref, c3_ref, token_ref, kv_out):
    copy_keys(got_ref, (c0_ref, c1_ref, c2_ref, c3_ref), kv_out)


def unpack_rest_kernel(
    got_ref, c0_ref, c1_ref, c2_ref, c3_ref, token_ref, q_out, kv_out
):
    for t in range(8):
        first = (7 - t) * 8 + 4 if t > 3 else t * 8
        q_out[t * 128:(t + 1) * 128, :] = got_ref[first:first + 4, 0].reshape(128, HD)
    copy_keys(got_ref, (c0_ref, c1_ref, c2_ref, c3_ref), kv_out)


def segment_of(t, yl, z0, c):
    low = t < 4
    s = yl * 16 + jnp.where(low, t, 7 - t) * 4 + z0 * 2 + c
    return jnp.where(low, s, 63 - s)


def bias_kernel(where_ref, mask_ref, own_out, near_out):
    yl, j, z0, c = where_ref[0], where_ref[1], where_ref[2], where_ref[3]
    mask = mask_ref[0].astype(jnp.float32).astype(jnp.bfloat16)
    r = lax.broadcasted_iota(jnp.int32, (32, 128), 0)
    qb = 2 * segment_of((r >> 1) & 7, yl, z0 ^ (r >> 4), c) + (r & 1)
    pick = (lax.broadcasted_iota(jnp.int32, (32, 128), 1) == qb).astype(jnp.float32)
    rows = jnp.dot(pick.astype(jnp.bfloat16), mask, preferred_element_type=jnp.float32)
    rows = rows.astype(jnp.bfloat16)

    def spread(block):
        n = block.shape[1]
        one = lax.broadcasted_iota(jnp.int32, (192, n), 0) == jnp.broadcast_to(block, (192, n))
        one = jnp.where(one, 1.0, 0.0).astype(jnp.bfloat16)
        return jnp.dot(rows, one, preferred_element_type=jnp.float32) > 0.5

    def span_bias(dy, dc):
        lane = lax.broadcasted_iota(jnp.int32, (1, 1024), 1)
        kb = 2 * segment_of(lane >> 7, yl ^ dy, z0, c ^ dc) + ((lane >> 6) & 1)
        ok = spread(kb + 64).astype(jnp.int32)
        q_full = jnp.broadcast_to(qb[:, :1], (32, 1024))
        k_full = jnp.broadcast_to(kb, (32, 1024))
        ok = ((k_full < q_full) & (ok != 0)) | (k_full == q_full)
        return jnp.where(ok, 0.0, neg_large)

    def cache_bias(dy, dc):
        lane = lax.broadcasted_iota(jnp.int32, (1, 512), 1)
        s = (yl ^ dy) * 16 + ((j - (lane >> 7)) & 3) * 4 + z0 * 2 + (c ^ dc)
        return jnp.where(spread(2 * s + ((lane >> 6) & 1)), 0.0, neg_large)

    for dy, out in enumerate((own_out, near_out)):
        for dc in range(2):
            out[:, dc * KEYS:dc * KEYS + 1024] = span_bias(dy, dc)
            out[:, dc * KEYS + 1024:(dc + 1) * KEYS] = cache_bias(dy, dc)


def score_tile(q, keys):
    return lax.dot_general(
        q, keys, (((1,), (1,)), ((), ())), preferred_element_type=jnp.float32
    )


def lane_sums(p):
    total = p[:, :HD]
    for i in range(1, p.shape[1] // HD):
        total = total + p[:, i * HD:(i + 1) * HD]
    return total


def attend(state, q, jobs, bias_ref, block):
    def scores(job):
        kv_ref, first = job[:2]
        return score_tile(q, kv_ref[0, first:first + 512, :])

    raws = [scores(jobs[0])]
    for n, (kv_ref, first, lanes, causal) in enumerate(jobs):
        if n + 1 < len(jobs):
            raws.append(scores(jobs[n + 1]))
        raw = raws[n] * score_scale
        parts = []
        for i in range(q.shape[0] // 64):
            bias = bias_ref[block + i:block + i + 1, lanes:lanes + 512]
            parts.append(raw[i * 64:(i + 1) * 64] + bias)
        s = jnp.concatenate(parts, axis=0)
        if causal:
            row = lax.broadcasted_iota(jnp.int32, s.shape, 0)
            col = lax.broadcasted_iota(jnp.int32, s.shape, 1)
            s = jnp.where(col <= row, s, neg_large)
        top, total, acc = state
        new_top = jnp.maximum(top, jnp.max(s, axis=1, keepdims=True))
        factor = jnp.exp2(top - new_top)
        p = jnp.exp2(s - new_top[:, :1])
        total = total * factor + lane_sums(p)
        acc = acc * factor + jnp.dot(
            p.astype(jnp.bfloat16),
            kv_ref[1, first:first + 512, :],
            preferred_element_type=jnp.float32,
        )
        state = new_top, total, acc
    return state


def fresh(rows):
    return (
        jnp.full((rows, HD), neg_large, jnp.float32),
        jnp.zeros((rows, HD), jnp.float32),
        jnp.zeros((rows, HD), jnp.float32),
    )


def own_kernel(which, q_ref, kv0, kv1, bias_ref, top, total, acc):
    for high in range(2):
        jobs = []
        for dc, kv_ref in enumerate((kv0, kv1)):
            lanes = dc * KEYS
            causal = which == 0 and dc == 0
            jobs.append((kv_ref, 1024, lanes + 1024, False))
            jobs.append((kv_ref, 0, lanes, causal and not high))
            if high:
                jobs.append((kv_ref, 512, lanes + 512, causal))
        rows = slice(high * 512, (high + 1) * 512)
        top[rows, :], total[rows, :], acc[rows, :] = attend(
            fresh(512), q_ref[rows, :], jobs, bias_ref, which * 16 + high * 8
        )


def near_fold(yl, which, q_ref, kv_refs, bias_ref, refs, done):
    def variant(firsts):
        for high in range(2):
            rows = slice(high * 512, (high + 1) * 512)
            jobs = [
                (kv_ref, first, dc * KEYS + first, False)
                for dc, kv_ref in kv_refs for first in firsts[high]
            ]
            state = attend(
                tuple(ref[rows, :] for ref in refs), q_ref[rows, :], jobs, bias_ref,
                which * 16 + high * 8,
            )
            done(high, *state)

    @pl.when(yl == 1)
    def _():
        variant(((0, 1024), (0, 1024)))

    @pl.when(yl == 0)
    def _():
        variant(((1024,), (0, 512, 1024)))


def to_row(column):
    row = lax.broadcasted_iota(jnp.int32, (128, HD), 0)
    col = lax.broadcasted_iota(jnp.int32, (128, HD), 1)
    return jnp.sum(jnp.where(row == col, column, 0.0), axis=0, keepdims=True)


def to_column(line):
    row = lax.broadcasted_iota(jnp.int32, (128, HD), 0)
    col = lax.broadcasted_iota(jnp.int32, (128, HD), 1)
    return jnp.sum(jnp.where(row == col, line, 0.0), axis=1, keepdims=True)


def near_partner_kernel(where_ref, q_ref, kv_ref, bias_ref, t_ref, l_ref, a_ref, part_out, levels):
    def done(high, top, total, acc):
        weight = jnp.sum(total, axis=1, keepdims=True)
        part_out[high * 512:(high + 1) * 512, :] = (acc / weight).astype(jnp.bfloat16)
        level = top + jnp.log2(jnp.broadcast_to(weight, (512, HD)))
        for i in range(4):
            t = high * 4 + i
            levels[t:t + 1, :] = to_row(level[i * 128:(i + 1) * 128])

    near_fold(
        where_ref[0], 1, q_ref, ((1, kv_ref),), bias_ref, (t_ref, l_ref, a_ref), done
    )
    rest = levels[...]
    pieces = []
    for _ in range(4):
        piece = rest.astype(jnp.bfloat16).astype(jnp.float32)
        rest = rest - piece
        pieces.append(piece)
    part_out[1024:, :] = jnp.concatenate(pieces, axis=0).astype(jnp.bfloat16)


def near_kernel(which, cores, where_ref, q_ref, *refs):
    def done(high, *state):
        rows = slice(high * 512, (high + 1) * 512)
        for ref, value in zip(refs[-3:], state):
            ref[rows, :] = value

    kv_refs = tuple(zip(cores, refs))
    refs = refs[len(cores):]
    near_fold(where_ref[0], which, q_ref, kv_refs, refs[0], refs[1:4], done)


def combine_kernel(top, total, acc, part_ref, extra_ref, out_ref):
    pieces = part_ref[1024:, :].astype(jnp.float32)
    levels = pieces[0:8] + (pieces[8:16] + (pieces[16:24] + pieces[24:32]))
    for t in range(8):
        rows = slice(t * 128, (t + 1) * 128)
        level = to_column(levels[t:t + 1])
        best = jnp.maximum(top[rows, :], level)
        factor = jnp.exp2(top[rows, :] - best)
        other = jnp.exp2(level - best)
        weight = jnp.sum(total[rows, :], axis=1, keepdims=True) * factor + other
        own = acc[rows, :] * factor + part_ref[rows, :].astype(jnp.float32) * other
        mixed = (own / weight + extra_ref[rows, :]).astype(jnp.bfloat16)
        to = t if t < 4 else 7 - t
        half = t // 4
        out_ref[to, half * 128:(half + 1) * 128, :] = mixed


def memory_kernel(where_ref, len_ref, gate_ref, q_ref, audio_ref, video_ref, out_ref):
    j = where_ref[1]
    slot = lax.broadcasted_iota(jnp.int32, (1, 512), 1)
    for high in range(2):
        q = q_ref[high * 512:(high + 1) * 512, :]
        mixed = jnp.zeros((512, HD), jnp.float32)
        raws = [score_tile(q, mem_ref[0]) for mem_ref in (audio_ref, video_ref)]
        for n, mem_ref in enumerate((audio_ref, video_ref)):
            bias = jnp.where(slot < len_ref[n], 0.0, neg_large)
            s = raws[n] * score_scale + bias
            p = jnp.exp2(s - jnp.max(s, axis=1, keepdims=True))
            total = jnp.sum(lane_sums(p), axis=1, keepdims=True)
            part = jnp.dot(
                p.astype(jnp.bfloat16), mem_ref[1], preferred_element_type=jnp.float32
            )
            gate = jnp.tanh(jnp.full((1, HD), gate_ref[n, j], jnp.float32))
            mixed = mixed + gate * (part / total)
        out_ref[high * 512:(high + 1) * 512, :] = mixed


def project_kernel(got_ref, w_ref, out_ref):
    mixed = jnp.concatenate([got_ref[j] for j in range(4)], axis=1)
    for n in range(4):
        cols = slice(n * 1024, (n + 1) * 1024)
        part = jnp.dot(mixed, w_ref[:, cols], preferred_element_type=jnp.float32)
        part = part.astype(jnp.bfloat16)
        for h in range(8):
            out_ref[h, :, cols] = part[h * 32:(h + 1) * 32]


def cost(us):
    return pl.CostEstimate(flops=int(us * 1.15e9), bytes_accessed=1024, transcendentals=0)


def after(array, token):
    def kernel(array_ref, token_ref, out_ref):
        pass

    return pl.pallas_call(
        kernel,
        out_shape=jax.ShapeDtypeStruct(array.shape, array.dtype),
        in_specs=[anywhere(), anywhere()],
        out_specs=anywhere(),
        input_output_aliases={0: 0},
        compiler_params=params(),
        cost_estimate=cost(0.001),
        name="after",
    )(array, token)


def f32(*shape):
    return jax.ShapeDtypeStruct(shape, jnp.float32)


def b16(*shape):
    return jax.ShapeDtypeStruct(shape, jnp.bfloat16)


def shards(
    span_qkv, cache_kv, audio_kv, video_kv, block_mask, mem_lengths, cross_gates, out_weight
):
    j = lax.axis_index("z2") * 2 + lax.axis_index("z1")
    where = jnp.stack(
        [lax.axis_index("yl"), j, lax.axis_index("z0"), lax.axis_index("c")]
    ).astype(jnp.int32)

    span_packed = pl.pallas_call(
        pack_kernel,
        out_shape=b16(32, 3, 32, HD),
        in_specs=[anywhere()],
        out_specs=anywhere(),
        scratch_shapes=[
            pltpu.VMEM((3, 32, 4096), jnp.bfloat16),
            pltpu.VMEM((32, 3, 32, HD), jnp.bfloat16),
            pltpu.SemaphoreType.DMA((4,)),
        ],
        compiler_params=params(60 * 2**20),
        cost_estimate=cost(2),
        name="pack",
    )(span_qkv)
    cache_packed = pl.pallas_call(
        pack_cache_kernel,
        out_shape=b16(4, 2, 128, HD),
        in_specs=[scalars(), whole(), anywhere()],
        out_specs=whole(),
        compiler_params=params(),
        cost_estimate=cost(1),
        name="pack_cache",
    )(where, cache_kv, span_packed)

    def swap(part, axis):
        return lax.ppermute(part, axis, xor_perm(2, 1))

    def swap_z(parts):
        return [parts[0]] + [lax.ppermute(parts[k], ZZ, turn_perm(4, k)) for k in range(1, 4)]

    own_bias, near_bias = pl.pallas_call(
        bias_kernel,
        out_shape=(f32(32, 2 * KEYS),) * 2,
        in_specs=[scalars(), whole()],
        out_specs=(whole(),) * 2,
        compiler_params=params(),
        cost_estimate=cost(2),
        name="bias",
    )(where, block_mask)

    got = lax.all_to_all(span_packed, ZZ + HEADS, split_axis=0, concat_axis=0, tiled=True)
    cache_own = swap_z([cache_packed[k] for k in range(4)])
    def unpack(kernel, token, name, *outs):
        return pl.pallas_call(
            kernel,
            out_shape=outs,
            in_specs=[whole()] * 5 + [anywhere()],
            out_specs=(whole(),) * len(outs),
            compiler_params=params(),
            cost_estimate=cost(0.001),
            name=name,
        )(got, *cache_own, token)

    (kv_sent,) = unpack(unpack_keys_kernel, own_bias, "unpack_keys", b16(2, KEYS, HD))
    kv_near = swap(kv_sent, "yl")
    queries, kv_own = unpack(
        unpack_rest_kernel, kv_sent, "unpack_rest", b16(1024, HD), b16(2, KEYS, HD)
    )
    partner_queries = swap(queries, "z0")
    sibling_keys = swap(kv_own, "c")

    extra = pl.pallas_call(
        memory_kernel,
        grid_spec=pltpu.PrefetchScalarGridSpec(
            num_scalar_prefetch=1,
            grid=(1,),
            in_specs=[
                scalars(),
                scalars(),
                pl.BlockSpec((1024, HD), lambda i, where: (0, 0)),
                pl.BlockSpec((2, 512, HD), lambda i, where: (0, 0, where[1])),
                pl.BlockSpec((2, 512, HD), lambda i, where: (0, 0, where[1])),
            ],
            out_specs=pl.BlockSpec((1024, HD), lambda i, where: (0, 0)),
        ),
        out_shape=f32(1024, HD),
        compiler_params=params(),
        cost_estimate=cost(0.001),
        name="memories",
    )(where, mem_lengths, cross_gates, queries, audio_kv, video_kv)

    def own(which, q):
        return pl.pallas_call(
            functools.partial(own_kernel, which),
            out_shape=(f32(1024, HD),) * 3,
            in_specs=[whole()] * 4,
            out_specs=(whole(),) * 3,
            compiler_params=params(),
            cost_estimate=cost(0.001),
            name="own_keys",
        )(q, kv_own, sibling_keys, own_bias)

    sibling_keys = after(sibling_keys, extra)
    states = [own(0, queries)]
    partner_queries = after(partner_queries, states[0][0])
    states.append(own(1, partner_queries))
    kv_near = after(kv_near, states[1][0])
    near_sibling = swap(kv_near, "c")

    def near(which, cores, q, keys, state):
        return pl.pallas_call(
            functools.partial(near_kernel, which, cores),
            out_shape=(f32(1024, HD),) * 3,
            in_specs=[scalars()] + [whole()] * (5 + len(cores)),
            out_specs=(whole(),) * 3,
            compiler_params=params(),
            cost_estimate=cost(2.5 * len(cores)),
            name="near_keys",
        )(where, q, *keys, near_bias, *state)

    state = near(1, (0,), partner_queries, (kv_near,), states[1])
    part = pl.pallas_call(
        near_partner_kernel,
        out_shape=b16(1056, HD),
        in_specs=[scalars()] + [whole()] * 6,
        out_specs=whole(),
        scratch_shapes=[pltpu.VMEM((8, HD), jnp.float32)],
        compiler_params=params(),
        cost_estimate=cost(3),
        name="near_keys_partner",
    )(where, partner_queries, near_sibling, near_bias, *state)
    part = swap(part, "z0")
    state = near(0, (0, 1), queries, (kv_near, near_sibling), states[0])
    state = pl.pallas_call(
        combine_kernel,
        out_shape=b16(4, 256, HD),
        in_specs=[whole()] * 5,
        out_specs=whole(),
        compiler_params=params(),
        cost_estimate=cost(1),
        name="combine",
    )(*state, part, extra)

    mixed = lax.all_to_all(state, ZZ, split_axis=0, concat_axis=0, tiled=True)
    partial_sums = pl.pallas_call(
        project_kernel,
        out_shape=b16(8, 32, 4096),
        in_specs=[whole()] * 2,
        out_specs=whole(),
        compiler_params=params(),
        cost_estimate=cost(3),
        name="project",
    )(mixed, out_weight)
    gathered = lax.all_to_all(partial_sums, HEADS, split_axis=0, concat_axis=0, tiled=True)
    return jnp.sum(gathered.astype(jnp.float32), axis=0).astype(jnp.bfloat16)


def solution(mesh):
    fine = Mesh(mesh.devices.reshape(SIZES), AXES)
    seq = ("yl", "z2", "z1", "z0", "c")
    placed = (
        P(None, seq + HEADS, None),
        P(None, seq, HEADS),
        P(None, None, HEADS),
        P(None, None, HEADS),
        P(HEADS, None, None),
        P(),
        P(None, HEADS),
        P(HEADS, None),
    )
    return jax.shard_map(
        shards, mesh=fine, in_specs=placed, out_specs=P(seq + HEADS, None), check_vma=False
    )
```

```python
import functools
import math

import jax
import jax.numpy as jnp
from jax import lax
from jax.experimental import pallas as pl
from jax.experimental.pallas import tpu as pltpu
from jax.sharding import Mesh
from jax.sharding import PartitionSpec as P

HD = 128
KEYS = 1536
neg_large = -1e30
score_scale = math.log2(math.e) / math.sqrt(HD)

AXES = ("yl", "z2", "z1", "z0", "c", "x", "yh")
SIZES = (2, 2, 2, 2, 2, 4, 2)
ZZ = ("z2", "z1")
HEADS = ("x", "yh")

VM = pltpu.VMEM
SM = pltpu.SMEM
whole = functools.partial(pl.BlockSpec, memory_space=VM)
anywhere = functools.partial(pl.BlockSpec, memory_space=pl.ANY)
scalars = functools.partial(pl.BlockSpec, memory_space=SM)


def params(vmem_limit_bytes=24 * 2**20):
    return pltpu.CompilerParams(vmem_limit_bytes=vmem_limit_bytes)


def xor_perm(count, k):
    return [(i, i ^ k) for i in range(count)]


def turn_perm(count, k):
    return [(i, (i + k) % count) for i in range(count)]


def pack_kernel(span_ref, cache_ref, span_out, *refs):
    cache_outs, (span_in, cache_in, packed, sems) = refs[:4], refs[4:]
    j = lax.axis_index("z2") * 2 + lax.axis_index("z1")
    reads = [
        pltpu.make_async_copy(span_ref.at[n], span_in.at[n], sems.at[n]) for n in range(3)
    ]
    reads.append(pltpu.make_async_copy(cache_ref, cache_in, sems.at[3]))
    for copy in reads:
        copy.start()
    for n in range(3):
        reads[n].wait()
        for d in range(32):
            col = ((d % 8) * 4 + d // 8) * HD
            packed[d, n] = span_in[n, :, col:col + HD]
    writes = [pltpu.make_async_copy(packed, span_out, sems.at[4])]
    writes[0].start()
    reads[3].wait()
    for k, cache_out in enumerate(cache_outs):
        piece = cache_in.at[:, :, pl.ds(pl.multiple_of(((j + k) & 3) * HD, HD), HD)]
        writes.append(pltpu.make_async_copy(piece, cache_out, sems.at[5 + k]))
        writes[1 + k].start()
    for copy in writes:
        copy.wait()


def copy_keys(got_ref, cache_refs, kv_out):
    for t in range(8):
        first = (7 - t) * 8 + 4 if t > 3 else t * 8
        rows = slice(t * 128, (t + 1) * 128)
        for n in range(2):
            kv_out[n, rows, :] = got_ref[first:first + 4, 1 + n].reshape(128, HD)
    for k, c_ref in enumerate(cache_refs):
        kv_out[:, 1024 + k * 128:1024 + (k + 1) * 128, :] = c_ref[...]


def unpack_keys_kernel(got_ref, c0_ref, c1_ref, c2_ref, c3_ref, token_ref, kv_out):
    copy_keys(got_ref, (c0_ref, c1_ref, c2_ref, c3_ref), kv_out)


def unpack_rest_kernel(
    got_ref, c0_ref, c1_ref, c2_ref, c3_ref, token_ref, q_out, kv_out
):
    for t in range(8):
        first = (7 - t) * 8 + 4 if t > 3 else t * 8
        q_out[t * 128:(t + 1) * 128, :] = got_ref[first:first + 4, 0].reshape(128, HD)
    copy_keys(got_ref, (c0_ref, c1_ref, c2_ref, c3_ref), kv_out)


def segment_of(t, yl, z0, c):
    low = t < 4
    s = yl * 16 + jnp.where(low, t, 7 - t) * 4 + z0 * 2 + c
    return jnp.where(low, s, 63 - s)


def bias_kernel(where_ref, mask_ref, own_out, near_out):
    yl, j, z0, c = where_ref[0], where_ref[1], where_ref[2], where_ref[3]
    mask = mask_ref[0].astype(jnp.float32).astype(jnp.bfloat16)
    r = lax.broadcasted_iota(jnp.int32, (32, 128), 0)
    qb = 2 * segment_of((r >> 1) & 7, yl, z0 ^ (r >> 4), c) + (r & 1)
    pick = (lax.broadcasted_iota(jnp.int32, (32, 128), 1) == qb).astype(jnp.float32)
    rows = jnp.dot(pick.astype(jnp.bfloat16), mask, preferred_element_type=jnp.float32)
    rows = rows.astype(jnp.bfloat16)

    def spread(block):
        n = block.shape[1]
        one = lax.broadcasted_iota(jnp.int32, (192, n), 0) == jnp.broadcast_to(block, (192, n))
        one = jnp.where(one, 1.0, 0.0).astype(jnp.bfloat16)
        return jnp.dot(rows, one, preferred_element_type=jnp.float32) > 0.5

    def span_bias(dy, dc):
        lane = lax.broadcasted_iota(jnp.int32, (1, 1024), 1)
        kb = 2 * segment_of(lane >> 7, yl ^ dy, z0, c ^ dc) + ((lane >> 6) & 1)
        ok = spread(kb + 64).astype(jnp.int32)
        q_full = jnp.broadcast_to(qb[:, :1], (32, 1024))
        k_full = jnp.broadcast_to(kb, (32, 1024))
        ok = ((k_full < q_full) & (ok != 0)) | (k_full == q_full)
        return jnp.where(ok, 0.0, neg_large)

    def cache_bias(dy, dc):
        lane = lax.broadcasted_iota(jnp.int32, (1, 512), 1)
        s = (yl ^ dy) * 16 + ((j - (lane >> 7)) & 3) * 4 + z0 * 2 + (c ^ dc)
        return jnp.where(spread(2 * s + ((lane >> 6) & 1)), 0.0, neg_large)

    for dy, out in enumerate((own_out, near_out)):
        for dc in range(2):
            out[:, dc * KEYS:dc * KEYS + 1024] = span_bias(dy, dc)
            out[:, dc * KEYS + 1024:(dc + 1) * KEYS] = cache_bias(dy, dc)


def score_tile(q, keys):
    return lax.dot_general(
        q, keys, (((1,), (1,)), ((), ())), preferred_element_type=jnp.float32
    )


def lane_sums(p):
    total = p[:, :HD]
    for i in range(1, p.shape[1] // HD):
        total = total + p[:, i * HD:(i + 1) * HD]
    return total


def attend(state, q, jobs, bias_ref, block):
    def scores(job):
        kv_ref, first = job[:2]
        return score_tile(q, kv_ref[0, first:first + 512, :])

    raws = [scores(jobs[0])]
    for n, (kv_ref, first, lanes, causal) in enumerate(jobs):
        if n + 1 < len(jobs):
            raws.append(scores(jobs[n + 1]))
        raw = raws[n] * score_scale
        parts = []
        for i in range(q.shape[0] // 64):
            bias = bias_ref[block + i:block + i + 1, lanes:lanes + 512]
            parts.append(raw[i * 64:(i + 1) * 64] + bias)
        s = jnp.concatenate(parts, axis=0)
        if causal:
            row = lax.broadcasted_iota(jnp.int32, s.shape, 0)
            col = lax.broadcasted_iota(jnp.int32, s.shape, 1)
            s = jnp.where(col <= row, s, neg_large)
        top, total, acc = state
        new_top = jnp.maximum(top, jnp.max(s, axis=1, keepdims=True))
        factor = jnp.exp2(top - new_top)
        p = jnp.exp2(s - new_top[:, :1])
        total = total * factor + lane_sums(p)
        acc = acc * factor + jnp.dot(
            p.astype(jnp.bfloat16),
            kv_ref[1, first:first + 512, :],
            preferred_element_type=jnp.float32,
        )
        state = new_top, total, acc
    return state


def fresh(rows):
    return (
        jnp.full((rows, HD), neg_large, jnp.float32),
        jnp.zeros((rows, HD), jnp.float32),
        jnp.zeros((rows, HD), jnp.float32),
    )


def own_kernel(which, q_ref, kv0, kv1, bias_ref, top, total, acc):
    for high in range(2):
        jobs = []
        for dc, kv_ref in enumerate((kv0, kv1)):
            lanes = dc * KEYS
            causal = which == 0 and dc == 0
            jobs.append((kv_ref, 1024, lanes + 1024, False))
            jobs.append((kv_ref, 0, lanes, causal and not high))
            if high:
                jobs.append((kv_ref, 512, lanes + 512, causal))
        rows = slice(high * 512, (high + 1) * 512)
        top[rows, :], total[rows, :], acc[rows, :] = attend(
            fresh(512), q_ref[rows, :], jobs, bias_ref, which * 16 + high * 8
        )


def near_fold(yl, which, q_ref, kv_refs, bias_ref, refs, done):
    def variant(firsts):
        for high in range(2):
            rows = slice(high * 512, (high + 1) * 512)
            jobs = [
                (kv_ref, first, dc * KEYS + first, False)
                for dc, kv_ref in kv_refs for first in firsts[high]
            ]
            state = attend(
                tuple(ref[rows, :] for ref in refs), q_ref[rows, :], jobs, bias_ref,
                which * 16 + high * 8,
            )
            done(high, *state)

    @pl.when(yl == 1)
    def _():
        variant(((0, 1024), (0, 1024)))

    @pl.when(yl == 0)
    def _():
        variant(((1024,), (0, 512, 1024)))


def to_row(column):
    row = lax.broadcasted_iota(jnp.int32, (128, HD), 0)
    col = lax.broadcasted_iota(jnp.int32, (128, HD), 1)
    return jnp.sum(jnp.where(row == col, column, 0.0), axis=0, keepdims=True)


def to_column(line):
    row = lax.broadcasted_iota(jnp.int32, (128, HD), 0)
    col = lax.broadcasted_iota(jnp.int32, (128, HD), 1)
    return jnp.sum(jnp.where(row == col, line, 0.0), axis=1, keepdims=True)


def near_partner_kernel(where_ref, q_ref, kv_ref, bias_ref, t_ref, l_ref, a_ref, part_out, levels):
    def done(high, top, total, acc):
        weight = jnp.sum(total, axis=1, keepdims=True)
        part_out[high * 512:(high + 1) * 512, :] = (acc / weight).astype(jnp.bfloat16)
        level = top + jnp.log2(jnp.broadcast_to(weight, (512, HD)))
        for i in range(4):
            t = high * 4 + i
            levels[t:t + 1, :] = to_row(level[i * 128:(i + 1) * 128])

    near_fold(
        where_ref[0], 1, q_ref, ((1, kv_ref),), bias_ref, (t_ref, l_ref, a_ref), done
    )
    rest = levels[...]
    pieces = []
    for _ in range(4):
        piece = rest.astype(jnp.bfloat16).astype(jnp.float32)
        rest = rest - piece
        pieces.append(piece)
    part_out[1024:, :] = jnp.concatenate(pieces, axis=0).astype(jnp.bfloat16)


def near_kernel(which, cores, where_ref, q_ref, *refs):
    def done(high, *state):
        rows = slice(high * 512, (high + 1) * 512)
        for ref, value in zip(refs[-3:], state):
            ref[rows, :] = value

    kv_refs = tuple(zip(cores, refs))
    refs = refs[len(cores):]
    near_fold(where_ref[0], which, q_ref, kv_refs, refs[0], refs[1:4], done)


def combine_kernel(top, total, acc, part_ref, extra_ref, out_ref):
    pieces = part_ref[1024:, :].astype(jnp.float32)
    levels = pieces[0:8] + (pieces[8:16] + (pieces[16:24] + pieces[24:32]))
    for t in range(8):
        rows = slice(t * 128, (t + 1) * 128)
        level = to_column(levels[t:t + 1])
        best = jnp.maximum(top[rows, :], level)
        factor = jnp.exp2(top[rows, :] - best)
        other = jnp.exp2(level - best)
        weight = jnp.sum(total[rows, :], axis=1, keepdims=True) * factor + other
        own = acc[rows, :] * factor + part_ref[rows, :].astype(jnp.float32) * other
        mixed = (own / weight + extra_ref[rows, :]).astype(jnp.bfloat16)
        to = t if t < 4 else 7 - t
        half = t // 4
        out_ref[to, half * 128:(half + 1) * 128, :] = mixed


def memory_kernel(where_ref, len_ref, gate_ref, q_ref, audio_ref, video_ref, out_ref):
    j = where_ref[1]
    slot = lax.broadcasted_iota(jnp.int32, (1, 512), 1)
    for high in range(2):
        q = q_ref[high * 512:(high + 1) * 512, :]
        mixed = jnp.zeros((512, HD), jnp.float32)
        raws = [score_tile(q, mem_ref[0]) for mem_ref in (audio_ref, video_ref)]
        for n, mem_ref in enumerate((audio_ref, video_ref)):
            bias = jnp.where(slot < len_ref[n], 0.0, neg_large)
            s = raws[n] * score_scale + bias
            p = jnp.exp2(s - jnp.max(s, axis=1, keepdims=True))
            total = jnp.sum(lane_sums(p), axis=1, keepdims=True)
            part = jnp.dot(
                p.astype(jnp.bfloat16), mem_ref[1], preferred_element_type=jnp.float32
            )
            gate = jnp.tanh(jnp.full((1, HD), gate_ref[n, j], jnp.float32))
            mixed = mixed + gate * (part / total)
        out_ref[high * 512:(high + 1) * 512, :] = mixed


def project_kernel(got_ref, w_ref, out_ref):
    mixed = jnp.concatenate([got_ref[j] for j in range(4)], axis=1)
    for n in range(4):
        cols = slice(n * 1024, (n + 1) * 1024)
        part = jnp.dot(mixed, w_ref[:, cols], preferred_element_type=jnp.float32)
        part = part.astype(jnp.bfloat16)
        for h in range(8):
            out_ref[h, :, cols] = part[h * 32:(h + 1) * 32]


def sum_kernel(got_ref, out_ref, sums, sems):
    writes = []
    for n in range(4):
        cols = slice(n * 1024, (n + 1) * 1024)
        total = got_ref[0, :, cols].astype(jnp.float32)
        for h in range(1, 8):
            total = total + got_ref[h, :, cols].astype(jnp.float32)
        sums[:, cols] = total.astype(jnp.bfloat16)
        writes.append(
            pltpu.make_async_copy(sums.at[:, cols], out_ref.at[:, cols], sems.at[n])
        )
        writes[n].start()
    for copy in writes:
        copy.wait()


def cost(us):
    return pl.CostEstimate(flops=int(us * 1.15e9), bytes_accessed=1024, transcendentals=0)


def after(array, token):
    def kernel(array_ref, token_ref, out_ref):
        pass

    return pl.pallas_call(
        kernel,
        out_shape=jax.ShapeDtypeStruct(array.shape, array.dtype),
        in_specs=[anywhere(), anywhere()],
        out_specs=anywhere(),
        input_output_aliases={0: 0},
        compiler_params=params(),
        cost_estimate=cost(0.001),
        name="after",
    )(array, token)


def f32(*shape):
    return jax.ShapeDtypeStruct(shape, jnp.float32)


def b16(*shape):
    return jax.ShapeDtypeStruct(shape, jnp.bfloat16)


def shards(
    span_qkv, cache_kv, audio_kv, video_kv, block_mask, mem_lengths, cross_gates, out_weight
):
    j = lax.axis_index("z2") * 2 + lax.axis_index("z1")
    where = jnp.stack(
        [lax.axis_index("yl"), j, lax.axis_index("z0"), lax.axis_index("c")]
    ).astype(jnp.int32)

    span_packed, *cache_packed = pl.pallas_call(
        pack_kernel,
        out_shape=(b16(32, 3, 32, HD),) + (b16(2, 128, HD),) * 4,
        in_specs=[anywhere()] * 2,
        out_specs=(anywhere(),) * 5,
        scratch_shapes=[
            pltpu.VMEM((3, 32, 4096), jnp.bfloat16),
            pltpu.VMEM((2, 128, 512), jnp.bfloat16),
            pltpu.VMEM((32, 3, 32, HD), jnp.bfloat16),
            pltpu.SemaphoreType.DMA((9,)),
        ],
        compiler_params=params(60 * 2**20),
        cost_estimate=cost(2),
        name="pack",
    )(span_qkv, cache_kv)

    def swap(part, axis):
        return lax.ppermute(part, axis, xor_perm(2, 1))

    def swap_z(parts):
        return [parts[0]] + [lax.ppermute(parts[k], ZZ, turn_perm(4, k)) for k in range(1, 4)]

    own_bias, near_bias = pl.pallas_call(
        bias_kernel,
        out_shape=(f32(32, 2 * KEYS),) * 2,
        in_specs=[scalars(), whole()],
        out_specs=(whole(),) * 2,
        compiler_params=params(),
        cost_estimate=cost(2),
        name="bias",
    )(where, block_mask)

    got = lax.all_to_all(span_packed, ZZ + HEADS, split_axis=0, concat_axis=0, tiled=True)
    cache_own = swap_z(cache_packed)
    def unpack(kernel, token, name, *outs):
        return pl.pallas_call(
            kernel,
            out_shape=outs,
            in_specs=[whole()] * 5 + [anywhere()],
            out_specs=(whole(),) * len(outs),
            compiler_params=params(),
            cost_estimate=cost(0.001),
            name=name,
        )(got, *cache_own, token)

    (kv_sent,) = unpack(unpack_keys_kernel, own_bias, "unpack_keys", b16(2, KEYS, HD))
    kv_near = swap(kv_sent, "yl")
    queries, kv_own = unpack(
        unpack_rest_kernel, kv_sent, "unpack_rest", b16(1024, HD), b16(2, KEYS, HD)
    )
    partner_queries = swap(queries, "z0")
    sibling_keys = swap(kv_own, "c")

    extra = pl.pallas_call(
        memory_kernel,
        grid_spec=pltpu.PrefetchScalarGridSpec(
            num_scalar_prefetch=1,
            grid=(1,),
            in_specs=[
                scalars(),
                scalars(),
                pl.BlockSpec((1024, HD), lambda i, where: (0, 0)),
                pl.BlockSpec((2, 512, HD), lambda i, where: (0, 0, where[1])),
                pl.BlockSpec((2, 512, HD), lambda i, where: (0, 0, where[1])),
            ],
            out_specs=pl.BlockSpec((1024, HD), lambda i, where: (0, 0)),
        ),
        out_shape=f32(1024, HD),
        compiler_params=params(),
        cost_estimate=cost(0.001),
        name="memories",
    )(where, mem_lengths, cross_gates, queries, audio_kv, video_kv)

    def own(which, q):
        return pl.pallas_call(
            functools.partial(own_kernel, which),
            out_shape=(f32(1024, HD),) * 3,
            in_specs=[whole()] * 4,
            out_specs=(whole(),) * 3,
            compiler_params=params(),
            cost_estimate=cost(0.001),
            name="own_keys",
        )(q, kv_own, sibling_keys, own_bias)

    sibling_keys = after(sibling_keys, extra)
    states = [own(0, queries)]
    partner_queries = after(partner_queries, states[0][0])
    states.append(own(1, partner_queries))
    kv_near = after(kv_near, states[1][0])
    near_sibling = swap(kv_near, "c")

    def near(which, cores, q, keys, state):
        return pl.pallas_call(
            functools.partial(near_kernel, which, cores),
            out_shape=(f32(1024, HD),) * 3,
            in_specs=[scalars()] + [whole()] * (5 + len(cores)),
            out_specs=(whole(),) * 3,
            compiler_params=params(),
            cost_estimate=cost(2.5 * len(cores)),
            name="near_keys",
        )(where, q, *keys, near_bias, *state)

    state = near(1, (0,), partner_queries, (kv_near,), states[1])
    part = pl.pallas_call(
        near_partner_kernel,
        out_shape=b16(1056, HD),
        in_specs=[scalars()] + [whole()] * 6,
        out_specs=whole(),
        scratch_shapes=[pltpu.VMEM((8, HD), jnp.float32)],
        compiler_params=params(),
        cost_estimate=cost(3),
        name="near_keys_partner",
    )(where, partner_queries, near_sibling, near_bias, *state)
    part = swap(part, "z0")
    state = near(0, (0, 1), queries, (kv_near, near_sibling), states[0])
    state = pl.pallas_call(
        combine_kernel,
        out_shape=b16(4, 256, HD),
        in_specs=[whole()] * 5,
        out_specs=whole(),
        compiler_params=params(),
        cost_estimate=cost(1),
        name="combine",
    )(*state, part, extra)

    mixed = lax.all_to_all(state, ZZ, split_axis=0, concat_axis=0, tiled=True)
    partial_sums = pl.pallas_call(
        project_kernel,
        out_shape=b16(8, 32, 4096),
        in_specs=[whole()] * 2,
        out_specs=whole(),
        compiler_params=params(),
        cost_estimate=cost(3),
        name="project",
    )(mixed, out_weight)
    gathered = lax.all_to_all(partial_sums, HEADS, split_axis=0, concat_axis=0, tiled=True)
    return pl.pallas_call(
        sum_kernel,
        out_shape=b16(32, 4096),
        in_specs=[whole()],
        out_specs=anywhere(),
        scratch_shapes=[
            pltpu.VMEM((32, 4096), jnp.bfloat16),
            pltpu.SemaphoreType.DMA((4,)),
        ],
        compiler_params=params(),
        cost_estimate=cost(1),
        name="sum",
    )(gathered)


def solution(mesh):
    fine = Mesh(mesh.devices.reshape(SIZES), AXES)
    seq = ("yl", "z2", "z1", "z0", "c")
    placed = (
        P(None, seq + HEADS, None),
        P(None, seq, HEADS),
        P(None, None, HEADS),
        P(None, None, HEADS),
        P(HEADS, None, None),
        P(),
        P(None, HEADS),
        P(HEADS, None),
    )
    return jax.shard_map(
        shards, mesh=fine, in_specs=placed, out_specs=P(seq + HEADS, None), check_vma=False
    )
```
